256 devices in a mesh: dp: 16 (over z, y_lo), cp: 16 (over x, y_hi, core).
Axes of the slice: x: 4, y: 4 (y_hi: 2, y_lo: 2; y = y_hi * 2 + y_lo), z: 8, core: 2. Of those that a mesh axis runs over, the one named last changes fastest.
Arguments:
- layer_input: bfloat16 [32768, 4096], P(('dp', 'cp')), may hold values from -0.75 to 0.75
- queries: bfloat16 [32768, 2048], P(('dp', 'cp')), may hold values from -6 to 6
- keys: bfloat16 [32768, 512], P(('dp', 'cp')), may hold values from -6 to 6
- values: bfloat16 [32768, 512], P(('dp', 'cp')), may hold values from -6 to 6
- outputs: bfloat16 [32768, 2048], P(('dp', 'cp')), may hold values from -6 to 6
- out_grad: bfloat16 [32768, 2048], P(('dp', 'cp')), may hold values from -1.5 to 1.5
- log_sum_exp: float32 [32768, 16], P(('dp', 'cp')), may hold values from 5 to 8
- group_first: int32 [16, 16], P('dp', 'cp'), may hold values from 0 to 12, as said below
- span_index: int32 [16, 16], P('dp', 'cp'), may hold values from 0 to 15, as said below
- seq_length: int32 [16, 16], P('dp', 'cp'), may hold values from 1 to 2048, as said below
Outputs:
- query_grad: bfloat16 [32768, 2048], P(('dp', 'cp'))
- weight_grad: bfloat16 [4096, 1024], P(('dp', 'cp'))
The draws below stay inside these ranges and needn't reach their ends.
Inputs may be any that keep to these rules, and one draw needn't show every extreme that they name: Each plan row cuts its 16 members into one to four contiguous groups, each beginning at a member whose index is a multiple of 4; group_first holds the first member of each member's group. Row 0 is always one group of all 16 members; in the last row the last 4 members always form a group of their own. `span_index`: within each group the span indices are a permutation of 0 to the group's size minus 1. `seq_length`: equal for all members of a group; for a group of m members it lies between (m - 1) * 128 + 1 and m * 128. Row 0's is 2048.
All inputs are finite; a program needn't handle non-finite values.
Results may differ from the reference program's by a relative error of at most 0.0062.
Values may be sent and summed in bfloat16 or wider, within the bound.
A program may use at most 128 MiB of HBM per device.

```python
import jax
import jax.numpy as jnp
from jax import lax

D = 4096
DH = 128
HQ = 16
HK = 4
TOK_DEV = 128
TOKENS = 32768
N_DP = 16
N_CP = 16


def plan_tables(key):
    cut_key = jax.random.fold_in(key, 11)
    order_key = jax.random.fold_in(key, 12)
    extra_key = jax.random.fold_in(key, 13)
    column = jnp.arange(N_CP, dtype=jnp.int32)
    row_ids = jnp.arange(N_DP, dtype=jnp.int32)
    row_zero = (row_ids == 0)[:, None]
    quarter = max(N_CP // 4, 1)
    cuts = (jax.random.randint(cut_key, (N_DP, N_CP), 0, 2) == 0) & (column % quarter == 0)[None, :]
    cuts = cuts | (column == 0)[None, :]
    cuts = cuts | (row_ids == N_DP - 1)[:, None] & (column == N_CP - quarter)[None, :]
    cuts = jnp.where(row_zero, (column == 0)[None, :], cuts)
    marks = jnp.where(cuts, column[None, :], 0).astype(jnp.int32)
    firsts = lax.cummax(marks, axis=1)
    sizes = jnp.sum((firsts[:, :, None] == firsts[:, None, :]).astype(jnp.int32), axis=-1)
    scores = firsts * (N_CP * 65536) + jax.random.randint(order_key, (N_DP, N_CP), 0, 65536) * N_CP + column[None, :]
    order = jnp.argsort(scores, axis=1)
    ranks = jnp.argsort(order, axis=1).astype(jnp.int32)
    spans = ranks - firsts
    extra = jax.random.randint(extra_key, (N_DP, N_CP), 1, TOK_DEV + 1)
    extra_group = jnp.take_along_axis(extra, firsts, axis=1)
    lengths = (sizes - 1) * TOK_DEV + extra_group
    lengths = jnp.where(row_zero, N_CP * TOK_DEV, lengths).astype(jnp.int32)
    return (firsts.astype(jnp.int32), spans.astype(jnp.int32), lengths)


def draw_group_first(key, part):
    tables = plan_tables(key)
    return tables[0]


def draw_span_index(key, part):
    tables = plan_tables(key)
    return tables[1]


def draw_seq_length(key, part):
    tables = plan_tables(key)
    return tables[2]


def with_spikes(entries, rng, source, target, parts, factor):
    owner, partner = [(jnp.arange(entries.shape[position]) // (entries.shape[position] // parts)).reshape([-1 if axis == position else 1 for axis in range(entries.ndim)]) for position in (source, target)]
    chosen = jax.random.permutation(rng, parts)[partner]
    strong = (owner == chosen) | (owner == (partner + parts // 2) % parts)
    return jnp.where(strong, factor * entries, entries)


def block_scale(rng, dims, pieces, least, high):
    loudness = 1.0
    for dim, blocks in pieces:
        heights = jax.random.uniform(jax.random.fold_in(jax.random.fold_in(rng, 6), dim), (blocks,), jnp.float32, least / len(pieces), high / len(pieces))
        loudness = loudness * jnp.repeat(jnp.exp(heights), dims[dim] // blocks).reshape((-1,) + (1,) * (len(dims) - 1 - dim))
    return loudness


def centred(rng, extent, deviation, limit, cuts=(), kind=jnp.bfloat16):
    factor_of = block_scale(rng, extent, cuts, -0.22, 0.18) if cuts else 1.0
    values = jax.random.normal(rng, extent, jnp.float32) * deviation * factor_of
    return jnp.minimum(jnp.maximum(values, -limit), limit).astype(kind)


def noise_with(own_key, dims, spread, most, cuts, heavy, kind=jnp.bfloat16):
    values = spread * jax.random.normal(own_key, dims, jnp.float32)
    if cuts:
        values = values * block_scale(own_key, dims, cuts, -0.22, 0.18)
    return jnp.clip(with_spikes(values, jax.random.fold_in(own_key, 3), *heavy), -most, most).astype(kind)


def setup_inputs(seed: int = 0) -> dict:
    key_of = jax.random.split(jax.random.key(seed), 11)
    return {
        "layer_input": noise_with(key_of[0], (TOKENS, D), 0.03, 0.75, ((0, 256),), (0, 1, 256, 6.0)),
        "queries": centred(key_of[1], (TOKENS, HQ * DH), 1.0, 6.0, ((0, 256),)),
        "keys": centred(key_of[2], (TOKENS, HK * DH), 1.0, 6.0, ((0, 256),)),
        "values": centred(key_of[3], (TOKENS, HK * DH), 1.0, 6.0, ((0, 256),)),
        "outputs": centred(key_of[4], (TOKENS, HQ * DH), 1.0, 6.0, ((0, 256),)),
        "out_grad": centred(key_of[5], (TOKENS, HQ * DH), 0.25, 1.5, ((0, 256),)),
        "log_sum_exp": jnp.clip(5.0 + 3.0 * jax.random.uniform(key_of[6], (TOKENS, HQ), jnp.float32) ** block_scale(key_of[6], (TOKENS, HQ), ((0, 256),), -0.2, 0.2), 5.0, 8.0),
        "group_first": draw_group_first(jax.random.fold_in(key_of[10], 71), 0),
        "span_index": draw_span_index(jax.random.fold_in(key_of[10], 71), 0),
        "seq_length": draw_seq_length(jax.random.fold_in(key_of[10], 71), 0),
    }


rope_base = 500000.0


def rope_back(grads, positions):
    half = DH // 2
    freq = rope_base ** (-(jnp.arange(half).astype(jnp.float32) * 2.0 / DH))
    angles = positions.astype(jnp.float32)[:, None] * freq[None, :]
    cosine = jnp.cos(angles)[:, None, :]
    sine = jnp.sin(angles)[:, None, :]
    lower = grads[..., :half]
    upper = grads[..., half:]
    return jnp.concatenate([lower * cosine + upper * sine, upper * cosine - lower * sine], axis=-1)


def reference(layer_input, queries, keys, values, outputs, out_grad, log_sum_exp, group_first, span_index, seq_length):
    row_tokens = N_CP * TOK_DEV
    group_width = HQ // HK
    scale_factor = 1.0 / (DH ** 0.5)

    def per_row(weight_acc, row_index):
        begin = (row_index * row_tokens).astype(jnp.int32)

        def cut(array):
            return lax.dynamic_slice_in_dim(array, begin, row_tokens, 0)

        firsts = jnp.repeat(lax.dynamic_index_in_dim(group_first, row_index, 0, False), TOK_DEV)
        spans = jnp.repeat(lax.dynamic_index_in_dim(span_index, row_index, 0, False), TOK_DEV)
        limits = jnp.repeat(lax.dynamic_index_in_dim(seq_length, row_index, 0, False), TOK_DEV)
        positions = spans * TOK_DEV + jnp.tile(jnp.arange(TOK_DEV, dtype=jnp.int32), N_CP)
        allowed = (firsts[:, None] == firsts[None, :]) & (positions[None, :] <= positions[:, None]) & (positions[:, None] < limits[:, None])
        query_f = cut(queries).astype(jnp.float32).reshape(row_tokens, HK, group_width, DH)
        grad_f = cut(out_grad).astype(jnp.float32).reshape(row_tokens, HK, group_width, DH)
        saved_f = cut(outputs).astype(jnp.float32).reshape(row_tokens, HK, group_width, DH)
        key_f = cut(keys).astype(jnp.float32).reshape(row_tokens, HK, DH)
        value_f = cut(values).astype(jnp.float32).reshape(row_tokens, HK, DH)
        lse_row = cut(log_sum_exp).reshape(row_tokens, HK, group_width).transpose(1, 2, 0)
        attn_scores = jnp.einsum('qhgd,khd->hgqk', query_f, key_f) * scale_factor
        attn_probs = jnp.exp(jnp.where(allowed[None, None], attn_scores - lse_row[..., None], -jnp.inf))
        probs_low = lax.optimization_barrier(attn_probs.astype(jnp.bfloat16)).astype(jnp.float32)
        grad_probs = jnp.einsum('qhgd,khd->hgqk', grad_f, value_f)
        row_delta = jnp.sum(grad_f * saved_f, axis=-1).transpose(1, 2, 0)
        grad_scores = attn_probs * (grad_probs - row_delta[..., None])
        scores_low = lax.optimization_barrier(grad_scores.astype(jnp.bfloat16)).astype(jnp.float32)
        query_grad = jnp.einsum('hgqk,khd->qhgd', scores_low, key_f) * scale_factor
        key_grad = jnp.einsum('hgqk,qhgd->khd', scores_low, query_f) * scale_factor
        value_grad = jnp.einsum('hgqk,qhgd->khd', probs_low, grad_f)
        key_plain = rope_back(key_grad, positions)
        kv_stack = jnp.concatenate([key_plain.reshape(row_tokens, HK * DH), value_grad.reshape(row_tokens, HK * DH)], axis=1).astype(jnp.bfloat16)
        weight_acc = weight_acc + lax.dot_general(cut(layer_input), kv_stack, (((0,), (0,)), ((), ())), preferred_element_type=jnp.float32)
        return weight_acc, query_grad.reshape(row_tokens, HQ * DH).astype(jnp.bfloat16)

    start_acc = jnp.zeros((D, 2 * HK * DH), jnp.float32)
    weight_acc, query_rows = lax.scan(per_row, start_acc, jnp.arange(N_DP, dtype=jnp.int32))
    return query_rows.reshape(TOKENS, HQ * DH), weight_acc.astype(jnp.bfloat16)
```

```python
import math

import jax
import jax.numpy as jnp
import numpy as np
from jax import lax
from jax.experimental import pallas as pl
from jax.experimental.pallas import tpu as pltpu
from jax.sharding import PartitionSpec as P

MESH = pl.DeviceIdType.MESH
F32 = jnp.float32
BF16 = jnp.bfloat16
ROPE_BASE = 500000.0
DH = 128
T = 128
N_CP = 16
N_DP = 16
SCALE = 1.0 / math.sqrt(DH)
LOG2E = math.log2(math.e)


def rope_tables():
    half = DH // 2
    freq = (ROPE_BASE ** (-(np.arange(half) * 2.0 / DH))).astype(np.float32)
    angles = (np.arange(N_CP * T, dtype=np.float32)[:, None] * freq[None, :]).astype(np.float32)
    cosine = np.cos(angles.astype(np.float64))
    sine = np.sin(angles.astype(np.float64))
    cos_table = np.concatenate([cosine, cosine], axis=1).astype(np.float32)
    sin_table = np.concatenate([sine, -sine], axis=1).astype(np.float32)
    return cos_table.reshape(N_CP, T, DH), sin_table.reshape(N_CP, T, DH)


def dot(a, b, ca, cb):
    return lax.dot_general(a, b, (((ca,), (cb,)), ((), ())), preferred_element_type=F32)


def kernel(
    x_hbm, q_hbm, k_hbm, v_hbm, o_hbm, g_hbm, lse_ref, first_ref, span_ref, length_ref, cos_hbm, sin_hbm,
    dq_out, w_out,
    x_v, o_v, g_v, cos_v, sin_v,
    qbuf, gbuf, kbuf, vbuf, stbuf, tagbuf, st_src, tag_src, tags_s, sig_s,
    qs, gs, ks, vs, kts, st_s, dqt, dkv_s,
    xts, xbuf, core_src, core_buf, rs_src, rs_buf, kvbuf,
    dq_s, dq_src, w_src, w_core, wsend, wbuf,
    lsem, asem_s, asem_r, xsem_s, xsem_r, ksem_s, ksem_r, wsem_s, wsem_r, dsem_s, dsem_r,
):
    r = lax.axis_index("dp")
    c = lax.axis_index("cp")
    x, y, q = c // 4, (c // 2) % 2, c % 2
    head = 8 * y + 2 * x + q
    mate = x * 4 + y * 2 + (1 - q)

    barrier = pltpu.get_barrier_semaphore()

    def greet_row(d, _):
        pl.semaphore_signal(barrier, inc=1, device_id=(r, (c + d) % N_CP), device_id_type=MESH)
        return 0

    lax.fori_loop(1, N_CP, greet_row, 0)

    def greet_far(i, _):
        rd = (r + 1 + i // 2) % N_DP
        cd = x * 4 + (i % 2) * 2 + q
        pl.semaphore_signal(barrier, inc=1, device_id=(rd, cd), device_id_type=MESH)
        return 0

    lax.fori_loop(0, 2 * (N_DP - 1), greet_far, 0)

    own = pl.ds(head * DH, DH)
    own_kv = pl.ds((head // 4) * DH, DH)
    loads = [
        pltpu.make_async_copy(o_hbm, o_v, lsem.at[0]),
        pltpu.make_async_copy(g_hbm, g_v, lsem.at[1]),
        pltpu.make_async_copy(x_hbm, x_v, lsem.at[2]),
        pltpu.make_async_copy(cos_hbm, cos_v, lsem.at[3]),
        pltpu.make_async_copy(sin_hbm, sin_v, lsem.at[4]),
        pltpu.make_async_copy(q_hbm.at[:, own], qbuf.at[c], lsem.at[5]),
        pltpu.make_async_copy(g_hbm.at[:, own], gbuf.at[c], lsem.at[6]),
        pltpu.make_async_copy(k_hbm.at[:, own_kv], kbuf.at[c], lsem.at[7]),
        pltpu.make_async_copy(v_hbm.at[:, own_kv], vbuf.at[c], lsem.at[8]),
    ]
    for load in loads:
        load.start()

    pl.semaphore_wait(barrier, (N_CP - 1) + 2 * (N_DP - 1))

    def row_peer(d):
        xd, yd, qd = (x + d // 4) % 4, (y + (d // 2) % 2) % 2, (q + d % 2) % 2
        return xd, yd, qd, xd * 4 + yd * 2 + qd

    def remote(src, dst, send, recv, rd, cd):
        return pltpu.make_async_remote_copy(
            src_ref=src, dst_ref=dst, send_sem=send, recv_sem=recv, device_id=(rd, cd), device_id_type=MESH
        )

    def take(ref, sem):
        pltpu.make_async_copy(ref, ref, sem).wait()

    def send_heads(d, _):
        xd, yd, qd, cd = row_peer(d)
        hd = 8 * yd + 2 * xd + qd
        cols = pl.ds(hd * DH, DH)
        kv_cols = pl.ds((hd // 4) * DH, DH)
        remote(q_hbm.at[:, cols], qbuf.at[c], asem_s.at[0], asem_r.at[0], r, cd).start()
        remote(k_hbm.at[:, kv_cols], kbuf.at[c], asem_s.at[1], asem_r.at[1], r, cd).start()
        remote(g_hbm.at[:, cols], gbuf.at[c], asem_s.at[2], asem_r.at[2], r, cd).start()
        remote(v_hbm.at[:, kv_cols], vbuf.at[c], asem_s.at[3], asem_r.at[3], r, cd).start()
        return 0

    lax.fori_loop(1, N_CP, send_heads, 0)

    first = first_ref[0, 0]
    span = span_ref[0, 0]
    length = length_ref[0, 0]
    row_id = lax.broadcasted_iota(jnp.int32, (8, T), 0)
    tag_src[...] = jnp.where(row_id == 0, first + span, jnp.where(row_id == 1, first, 0))
    pos = span * T + lax.broadcasted_iota(jnp.int32, (1, T), 1)
    low = jnp.where(pos < length, first * T, 2 * N_CP * T).astype(F32)
    lse_t = jnp.concatenate([lse_ref[...] * LOG2E, jnp.zeros((T, T - 16), F32)], axis=1).T
    for load in loads[:2]:
        load.wait()
    lane = lax.broadcasted_iota(jnp.int32, (T, T), 1)
    delta = jnp.zeros((T, T), F32)
    for h in range(16):
        cols = slice(h * DH, (h + 1) * DH)
        part = jnp.sum(o_v[:, cols].astype(F32) * g_v[:, cols].astype(F32), axis=1, keepdims=True)
        delta = jnp.where(lane == h, part, delta)
    delta_t = delta.T
    for h in range(16):
        rows = jnp.concatenate([lse_t[h : h + 1], delta_t[h : h + 1], low, jnp.zeros((5, T), F32)], axis=0)
        st_src[h] = rows

    def send_stats(d, _):
        xd, yd, qd, cd = row_peer(d)
        hd = 8 * yd + 2 * xd + qd
        remote(st_src.at[hd], stbuf.at[c], asem_s.at[4], asem_r.at[4], r, cd).start()
        remote(tag_src, tagbuf.at[c], asem_s.at[5], asem_r.at[5], r, cd).start()
        return 0

    lax.fori_loop(1, N_CP, send_stats, 0)
    stbuf[c] = st_src[head]
    tagbuf[c] = tag_src[...]

    loads[2].wait()

    def turn_x(b, _):
        for part in range(2):
            block = x_v[:, pl.ds(pl.multiple_of(b * 256 + part * 128, 128), 128)].T
            for k in range(8):
                owner = part * 8 + k
                start = (owner % 2) * 512 + ((owner // 2) % 2) * 256 + b * 16
                xts[owner // 4, pl.ds(pl.multiple_of(start, 16), 16), :] = block[k * 16 : (k + 1) * 16]
        return 0

    lax.fori_loop(0, N_DP, turn_x, 0)

    for load in loads[3:]:
        load.wait()
    for i, buf in enumerate((qbuf, kbuf, gbuf, vbuf, stbuf, tagbuf)):
        take(buf.at[pl.ds(0, N_CP - 1)], asem_r.at[i])

    slot_u, slot_m = x // 2, (x % 2) * 2 + y

    def send_x(d, _):
        xd, yd = (x + d // 2) % 4, (y + d % 2) % 2
        dst = xbuf.at[slot_u, :, pl.ds(pl.multiple_of(slot_m * T, T), T)]
        remote(xts.at[xd], dst, xsem_s, xsem_r, r, xd * 4 + yd * 2 + q).start()
        return 0

    lax.fori_loop(1, 8, send_x, 0)
    keep = pltpu.make_async_copy(
        xts.at[x], xbuf.at[slot_u, :, pl.ds(pl.multiple_of(slot_m * T, T), T)], lsem.at[0]
    )
    keep.start()

    tag_load = pltpu.make_async_copy(tagbuf, tags_s, lsem.at[1])
    tag_load.start()
    tag_load.wait()
    place = [tags_s[m, 0, 0] for m in range(N_CP)]
    for p in range(N_CP):
        m = jnp.int32(0)
        for i in range(1, N_CP):
            m = jnp.where(place[i] == p, i, m)
        sig_s[p] = p - tags_s[m, 1, 0]
        qs[p] = qbuf[m]
        gs[p] = gbuf[m]
        vs[p] = vbuf[m]
        key = kbuf[m]
        ks[p] = key
        kts[p // 2, :, (p % 2) * T : (p % 2 + 1) * T] = key.T
        st_s[p // 2, :, (p % 2) * T : (p % 2 + 1) * T] = stbuf[m]
    dqt[...] = jnp.zeros_like(dqt)

    def key_block(step, _):
        kb = 7 - step
        key = ks[pl.ds(2 * kb, 2)].reshape(256, DH)
        value = vs[pl.ds(2 * kb, 2)].reshape(256, DH)
        key_t = kts[kb]

        def unit(qb, carry, diagonal):
            dk, dv = carry
            query = qs[pl.ds(2 * qb, 2)].reshape(256, DH)
            grad = gs[pl.ds(2 * qb, 2)].reshape(256, DH)
            stats = st_s[qb]
            scores = dot(key, query, 1, 1)
            dp = dot(value, grad, 1, 1)
            s_at = lax.broadcasted_iota(jnp.int32, (256, 256), 0)
            allowed = s_at >= stats[2:3].astype(jnp.int32) - kb * 256
            if diagonal:
                allowed = allowed & (s_at <= lax.broadcasted_iota(jnp.int32, (256, 256), 1))
            probs = jnp.where(allowed, jnp.exp2(scores * (SCALE * LOG2E) - stats[0:1]), 0.0)
            ds = (probs * (dp - stats[1:2])).astype(BF16)
            dv = dv + dot(probs.astype(BF16), grad, 1, 0)
            dk = dk + dot(ds, query, 1, 0)
            dqt[qb] += dot(key_t, ds, 1, 0)
            return dk, dv

        zero = jnp.zeros((256, DH), F32)
        carry = unit(kb, (zero, zero), True)
        dk, dv = lax.fori_loop(kb + 1, 8, lambda qb, cc: unit(qb, cc, False), carry)
        for i in range(2):
            p = 2 * kb + i
            rows = slice(i * T, (i + 1) * T)
            turned = dk[rows] * SCALE
            sig = sig_s[p]
            plain = turned * cos_v[sig] + pltpu.roll(turned, DH // 2, 1) * sin_v[sig]
            dkv_s[p] = jnp.concatenate([plain, dv[rows]], axis=1).astype(BF16)
        return 0

    lax.fori_loop(0, 8, key_block, 0)

    for e in range(8):
        core_src[e] = dkv_s[tags_s[2 * e + (1 - q), 0, 0]]
    to_mate = remote(core_src, core_buf, ksem_s.at[0], ksem_r.at[0], r, mate)
    to_mate.start()

    for p in range(N_CP):
        dq_s[p] = (dqt[p // 2, :, (p % 2) * T : (p % 2 + 1) * T] * SCALE).T.astype(BF16)
    for m in range(N_CP):
        dq_src[m] = dq_s[place[m]]

    to_mate.wait()
    g, u = x // 2, x % 2
    for e in range(4):
        give = 4 * (1 - u) + e
        summed = dkv_s[tags_s[2 * give + q, 0, 0]].astype(F32) + core_buf[give].astype(F32)
        rs_src[e] = summed.astype(BF16)
    pair = (x // 2) * 2 + (1 - u)
    to_pair = remote(rs_src, rs_buf, ksem_s.at[1], ksem_r.at[1], r, pair * 4 + y * 2 + q)
    to_pair.start()
    to_pair.wait()
    for e in range(4):
        mine = 4 * u + e
        summed = dkv_s[tags_s[2 * mine + q, 0, 0]].astype(F32) + core_buf[mine].astype(F32)
        kvbuf[x, pl.ds(e * T, T), :] = (summed + rs_buf[e].astype(F32)).astype(BF16)
    shares = []
    for d in range(1, 4):
        cd = ((x + d) % 4) * 4 + y * 2 + q
        share = remote(kvbuf.at[x], kvbuf.at[x], ksem_s.at[1 + d], ksem_r.at[1 + d], r, cd)
        share.start()
        shares.append(share)

    def send_dq(d, _):
        xd, yd, qd, cd = row_peer(d)
        remote(dq_src.at[cd], dq_out.at[:, own], dsem_s, dsem_r, r, cd).start()
        return 0

    lax.fori_loop(1, N_CP, send_dq, 0)
    dq_keep = pltpu.make_async_copy(dq_src.at[c], dq_out.at[:, own], lsem.at[2])
    dq_keep.start()

    take(xbuf.at[:, pl.ds(0, 7 * T), :], xsem_r)
    keep.wait()
    for share in shares:
        share.wait()

    def tile(start, gg):
        rows = pl.ds(pl.multiple_of(start, 256), 256)
        return dot(xbuf[0, rows, :], kvbuf[2 * gg], 1, 0) + dot(xbuf[1, rows, :], kvbuf[2 * gg + 1], 1, 0)

    for yo in range(2):
        for gg in range(2):
            w_src[yo * 256 : (yo + 1) * 256, gg * 256 : (gg + 1) * 256] = tile(
                (1 - q) * 512 + yo * 256, gg
            ).astype(BF16)
    w_mate = remote(w_src, w_core, wsem_s.at[0], wsem_r.at[0], r, mate)
    w_mate.start()
    w_mate.wait()
    for yo in range(2):
        for gg in range(2):
            block = tile(q * 512 + yo * 256, gg) + w_core[
                yo * 256 : (yo + 1) * 256, gg * 256 : (gg + 1) * 256
            ].astype(F32)
            wsend[yo, :, :, gg * 256 : (gg + 1) * 256] = block.astype(BF16).reshape(N_DP, 16, 256)

    def send_w(i, _):
        rd, yd = (r + i // 2) % N_DP, (y + i % 2) % 2
        remote(wsend.at[yd, rd], wbuf.at[2 * r + y], wsem_s.at[1], wsem_r.at[1], rd, x * 4 + yd * 2 + q).start()
        return 0

    lax.fori_loop(1, 2 * N_DP, send_w, 0)
    wbuf[2 * r + y] = wsend[y, r]
    take(wbuf.at[pl.ds(0, 2 * N_DP - 1)], wsem_r.at[1])
    for yy in range(2):
        total = lax.fori_loop(
            1, N_DP, lambda i, t: t + wbuf[2 * i + yy].astype(F32), wbuf[yy].astype(F32)
        )
        for gg in range(2):
            j = 2 * yy + gg
            w_out[:, j * DH : (j + 1) * DH] = total[:, gg * 256 : gg * 256 + DH].astype(BF16)
            w_out[:, 512 + j * DH : 512 + (j + 1) * DH] = total[:, gg * 256 + DH : (gg + 1) * 256].astype(BF16)

    take(dq_src.at[pl.ds(0, N_CP - 1)], dsem_r)
    take(dq_src.at[pl.ds(0, N_CP - 1)], dsem_s)
    dq_keep.wait()
    for i, buf in enumerate((qbuf, kbuf, gbuf, vbuf, stbuf, tagbuf)):
        take(buf.at[pl.ds(0, N_CP - 1)], asem_s.at[i])
    take(xbuf.at[:, pl.ds(0, 7 * T), :], xsem_s)
    take(wbuf.at[pl.ds(0, 2 * N_DP - 1)], wsem_s.at[1])


def shards(layer_input, queries, keys, values, outputs, out_grad, log_sum_exp, group_first, span_index, seq_length):
    cos_table, sin_table = rope_tables()
    anywhere = pl.BlockSpec(memory_space=pl.ANY)
    vmem = pl.BlockSpec(memory_space=pltpu.VMEM)
    smem = pl.BlockSpec(memory_space=pltpu.SMEM)
    dma = pltpu.SemaphoreType.DMA
    V = pltpu.VMEM
    scratch = [
        V((T, 4096), BF16), V((T, 2048), BF16), V((T, 2048), BF16), V((16, T, DH), F32), V((16, T, DH), F32),
        V((16, T, DH), BF16), V((16, T, DH), BF16), V((16, T, DH), BF16), V((16, T, DH), BF16),
        V((16, 8, T), F32), V((16, 8, T), jnp.int32), V((16, 8, T), F32), V((8, T), jnp.int32),
        pltpu.SMEM((16, 8, T), jnp.int32), pltpu.SMEM((16,), jnp.int32),
        V((16, T, DH), BF16), V((16, T, DH), BF16), V((16, T, DH), BF16), V((16, T, DH), BF16),
        V((8, DH, 256), BF16), V((8, 8, 256), F32), V((8, DH, 256), F32), V((16, T, 256), BF16),
        V((4, 1024, T), BF16), V((2, 1024, 512), BF16), V((8, T, 256), BF16), V((8, T, 256), BF16),
        V((4, T, 256), BF16), V((4, T, 256), BF16), V((4, 512, 256), BF16),
        V((16, T, DH), BF16), V((16, T, DH), BF16), V((512, 512), BF16), V((512, 512), BF16),
        V((2, 16, 16, 512), BF16), V((32, 16, 512), BF16),
        dma((9,)), dma((6,)), dma((6,)), dma, dma, dma((5,)), dma((5,)), dma((2,)), dma((2,)), dma, dma,
    ]
    return pl.pallas_call(
        kernel,
        out_shape=(
            jax.ShapeDtypeStruct((T, 2048), BF16),
            jax.ShapeDtypeStruct((16, 1024), BF16),
        ),
        in_specs=[anywhere] * 6 + [vmem, smem, smem, smem, anywhere, anywhere],
        out_specs=(anywhere, vmem),
        scratch_shapes=scratch,
        compiler_params=pltpu.CompilerParams(
            collective_id=0, has_side_effects=True, vmem_limit_bytes=48 * 1024 * 1024
        ),
        name="attention_backward",
    )(
        layer_input, queries, keys, values, outputs, out_grad, log_sum_exp,
        group_first, span_index, seq_length, jnp.asarray(cos_table), jnp.asarray(sin_table),
    )


def solution(mesh):
    both = P(("dp", "cp"), None)
    placed = (both,) * 7 + (P("dp", "cp"),) * 3
    return jax.shard_map(shards, mesh=mesh, in_specs=placed, out_specs=(both, both), check_vma=False)
```

```python
import math

import jax
import jax.numpy as jnp
import numpy as np
from jax import lax
from jax.experimental import pallas as pl
from jax.experimental.pallas import tpu as pltpu
from jax.sharding import PartitionSpec as P

MESH = pl.DeviceIdType.MESH
F32 = jnp.float32
BF16 = jnp.bfloat16
ROPE_BASE = 500000.0
DH = 128
T = 128
N_CP = 16
N_DP = 16
SCALE = 1.0 / math.sqrt(DH)
LOG2E = math.log2(math.e)
NT = 4
BL = NT * T
NB = N_CP // NT
ORDER = (6, 14, 10, 2, 4, 12, 8, 3, 7, 15, 11, 5, 13, 9, 1)
FAR = (4, 3, 5, 2, 6, 1, 7)


def rope_tables():
    half = DH // 2
    freq = (ROPE_BASE ** (-(np.arange(half) * 2.0 / DH))).astype(np.float32)
    angles = (np.arange(N_CP * T, dtype=np.float32)[:, None] * freq[None, :]).astype(np.float32)
    cosine = np.cos(angles.astype(np.float64))
    sine = np.sin(angles.astype(np.float64))
    cos_table = np.concatenate([cosine, cosine], axis=1).astype(np.float32)
    sin_table = np.concatenate([sine, -sine], axis=1).astype(np.float32)
    return cos_table.reshape(N_CP, T, DH), sin_table.reshape(N_CP, T, DH)


def dot(a, b, ca, cb):
    return lax.dot_general(a, b, (((ca,), (cb,)), ((), ())), preferred_element_type=F32)


def kernel(
    x_hbm, q_hbm, k_hbm, v_hbm, o_hbm, g_hbm, lse_ref, first_ref, span_ref, length_ref, cos_hbm, sin_hbm,
    dq_out, w_out,
    x_v, o_v, g_v, cos_v, sin_v,
    qbuf, gbuf, kvbuf_in, stbuf, tagbuf, st_src, tag_src, tags_s, sig_s,
    qs, gs, kvs, kts, st_s, dqt, dkv_s,
    xts, xbuf, core_src, core_buf, rs_src, rs_buf, kvbuf,
    dq_s, dq_src, w_src, w_core, w_own, wsend, wbuf, wsum, wpart,
    lsem, asem_s, asem_r, xsem_s, xsem_r, ksem_s, ksem_r, wsem_s, wsem_r, dsem_s, dsem_r,
):
    r = lax.axis_index("dp")
    c = lax.axis_index("cp")
    x, y, q = c // 4, (c // 2) % 2, c % 2
    head = 8 * y + 2 * x + q
    mate = x * 4 + y * 2 + (1 - q)

    barrier = pltpu.get_barrier_semaphore()
    z, low_y = r // 2, r % 2
    beside = z * 2 + 1 - low_y
    y_mate = x * 4 + (1 - y) * 2 + q

    def greet(rd, cd):
        pl.semaphore_signal(barrier, inc=1, device_id=(rd, cd), device_id_type=MESH)

    for d in range(1, N_CP):
        greet(r, (c + d) % N_CP)
    for dz in FAR:
        greet(((z + dz) % 8) * 2 + low_y, c)
    greet(beside, c)
    greet(beside, y_mate)

    own = pl.ds(head * DH, DH)
    own_kv = pl.ds((head // 4) * DH, DH)
    kv_hbm = (k_hbm, v_hbm)
    loads = [
        pltpu.make_async_copy(o_hbm, o_v, lsem.at[0]),
        pltpu.make_async_copy(g_hbm, g_v, lsem.at[1]),
        pltpu.make_async_copy(x_hbm, x_v, lsem.at[2]),
        pltpu.make_async_copy(cos_hbm, cos_v, lsem.at[3]),
        pltpu.make_async_copy(sin_hbm, sin_v, lsem.at[4]),
        pltpu.make_async_copy(q_hbm.at[:, own], qbuf.at[c], lsem.at[5]),
        pltpu.make_async_copy(g_hbm.at[:, own], gbuf.at[c], lsem.at[6]),
    ]
    for load in loads:
        load.start()
    for core in range(2):

        @pl.when(q == core)
        def _():
            pltpu.make_async_copy(kv_hbm[core].at[:, own_kv], kvbuf_in.at[c], lsem.at[7]).start()

    pl.semaphore_wait(barrier, (N_CP - 1) + len(FAR) + 2)

    def row_peer(d):
        xd, yd, qd = (x + d // 4) % 4, (y + (d // 2) % 2) % 2, (q + d % 2) % 2
        return xd, yd, qd, xd * 4 + yd * 2 + qd

    def remote(src, dst, send, recv, rd, cd):
        return pltpu.make_async_remote_copy(
            src_ref=src, dst_ref=dst, send_sem=send, recv_sem=recv, device_id=(rd, cd), device_id_type=MESH
        )

    def take(ref, sem):
        pltpu.make_async_copy(ref, ref, sem).wait()

    first = first_ref[0, 0]
    span = span_ref[0, 0]
    length = length_ref[0, 0]
    row_id = lax.broadcasted_iota(jnp.int32, (8, T), 0)
    tag_src[...] = jnp.where(row_id == 0, first + span, jnp.where(row_id == 1, first, 0))
    for d in ORDER:
        xd, yd, qd, cd = row_peer(d)
        kv_cols = pl.ds((2 * yd + xd // 2) * DH, DH)
        for core in range(2):

            @pl.when(qd == core)
            def _():
                remote(kv_hbm[core].at[:, kv_cols], kvbuf_in.at[c], asem_s.at[1], asem_r.at[1], r, cd).start()

        remote(tag_src, tagbuf.at[c], asem_s.at[4], asem_r.at[4], r, cd).start()

    def send_heads(ref, buf, i):
        for d in ORDER:
            xd, yd, qd, cd = row_peer(d)
            cols = pl.ds((8 * yd + 2 * xd + qd) * DH, DH)
            remote(ref.at[:, cols], buf.at[c], asem_s.at[i], asem_r.at[i], r, cd).start()

    send_heads(q_hbm, qbuf, 0)

    pos = span * T + lax.broadcasted_iota(jnp.int32, (1, T), 1)
    low = jnp.where(pos < length, first * T, 2 * N_CP * T).astype(F32)
    lse_t = jnp.concatenate([lse_ref[...] * LOG2E, jnp.zeros((T, T - 16), F32)], axis=1).T
    for load in loads[:2]:
        load.wait()
    lane = lax.broadcasted_iota(jnp.int32, (T, T), 1)
    delta = jnp.zeros((T, T), F32)
    for h in range(16):
        cols = slice(h * DH, (h + 1) * DH)
        part = jnp.sum(o_v[:, cols].astype(F32) * g_v[:, cols].astype(F32), axis=1, keepdims=True)
        delta = jnp.where(lane == h, part, delta)
    delta_t = delta.T
    for h in range(16):
        rows = jnp.concatenate([lse_t[h : h + 1], delta_t[h : h + 1], low, jnp.zeros((5, T), F32)], axis=0)
        st_src[h] = rows

    def send_stats(d, _):
        xd, yd, qd, cd = row_peer(d)
        hd = 8 * yd + 2 * xd + qd
        remote(st_src.at[hd], stbuf.at[c], asem_s.at[3], asem_r.at[3], r, cd).start()
        return 0

    lax.fori_loop(1, N_CP, send_stats, 0)
    send_heads(g_hbm, gbuf, 2)
    stbuf[c] = st_src[head]
    tagbuf[c] = tag_src[...]

    loads[2].wait()

    def turn_x(b, _):
        for part in range(2):
            block = x_v[:, pl.ds(pl.multiple_of(b * 256 + part * 128, 128), 128)].T
            for k in range(8):
                owner = part * 8 + k
                start = (owner % 2) * 512 + ((owner // 2) % 2) * 256 + b * 16
                xts[owner // 4, pl.ds(pl.multiple_of(start, 16), 16), :] = block[k * 16 : (k + 1) * 16]
        return 0

    lax.fori_loop(0, N_DP, turn_x, 0)

    take(tagbuf.at[pl.ds(0, N_CP - 1)], asem_r.at[4])
    tag_load = pltpu.make_async_copy(tagbuf, tags_s, lsem.at[8])
    tag_load.start()
    tag_load.wait()
    place = [tags_s[m, 0, 0] for m in range(N_CP)]
    member = []
    for p in range(N_CP):
        m = jnp.int32(0)
        for i in range(1, N_CP):
            m = jnp.where(place[i] == p, i, m)
        member.append(m)
        sig_s[p] = p - tags_s[m, 1, 0]

    pltpu.make_async_copy(kvbuf_in.at[c], kvbuf_in.at[c], lsem.at[7]).wait()
    take(kvbuf_in.at[pl.ds(0, N_CP - 1)], asem_r.at[1])
    for p in range(N_CP):
        kvs[q, p] = kvbuf_in[member[p]]
    forward = remote(kvs.at[q], kvs.at[q], lsem.at[9], lsem.at[10], r, mate)
    forward.start()

    for load in loads[3:]:
        load.wait()
    for i, buf in ((0, qbuf), (2, gbuf), (3, stbuf)):
        take(buf.at[pl.ds(0, N_CP - 1)], asem_r.at[i])

    def x_slot(xs, ys):
        lanes = pl.ds(pl.multiple_of(((xs % 2) * 2 + ys) * T, T), T)
        return xbuf.at[xs // 2, :, lanes]

    x_sends = []
    for i, d in enumerate((1, 3, 2)):
        send = remote(xts.at[(x + d) % 4], x_slot(x, y), xsem_s.at[i], xsem_r.at[i], r, ((x + d) % 4) * 4 + y * 2 + q)
        send.start()
        x_sends.append(send)
    keep = pltpu.make_async_copy(xts.at[x], x_slot(x, y), lsem.at[0])
    keep.start()
    across = [remote(xts.at[x], x_slot(x, y), xsem_s.at[3], xsem_r.at[3], r, y_mate)]
    across[0].start()

    def hand_on(i):
        slot = x_slot((x - (1, 3, 2)[i]) % 4, y)
        x_sends[i].wait_recv()
        across.append(remote(slot, slot, xsem_s.at[4 + i], xsem_r.at[4 + i], r, y_mate))
        across[-1].start()

    for p in range(N_CP):
        qs[p] = qbuf[member[p]]
        gs[p] = gbuf[member[p]]
        st_s[p // NT, :, (p % NT) * T : (p % NT + 1) * T] = stbuf[member[p]]
    forward.wait()
    for p in range(N_CP):
        kts[p // NT, :, (p % NT) * T : (p % NT + 1) * T] = kvs[0, p].T
    dqt[...] = jnp.zeros_like(dqt)

    def key_block(step, _):
        kb = NB - 1 - step
        key = kvs[0, pl.ds(NT * kb, NT)].reshape(BL, DH)
        value = kvs[1, pl.ds(NT * kb, NT)].reshape(BL, DH)
        key_t = kts[kb]

        def unit(qb, carry, diagonal):
            dk, dv = carry
            query = qs[pl.ds(NT * qb, NT)].reshape(BL, DH)
            grad = gs[pl.ds(NT * qb, NT)].reshape(BL, DH)
            stats = st_s[qb]
            scores = dot(key, query, 1, 1)
            dp = dot(value, grad, 1, 1)
            s_at = lax.broadcasted_iota(jnp.int32, (BL, BL), 0)
            allowed = s_at >= stats[2:3].astype(jnp.int32) - kb * BL
            if diagonal:
                allowed = allowed & (s_at <= lax.broadcasted_iota(jnp.int32, (BL, BL), 1))
            probs = jnp.where(allowed, jnp.exp2(scores * (SCALE * LOG2E) - stats[0:1]), 0.0)
            ds = (probs * (dp - stats[1:2])).astype(BF16)
            dv = dv + dot(probs.astype(BF16), grad, 1, 0)
            dk = dk + dot(ds, query, 1, 0)
            dqt[qb] += dot(key_t, ds, 1, 0)
            return dk, dv

        zero = jnp.zeros((BL, DH), F32)
        carry = unit(kb, (zero, zero), True)
        dk, dv = lax.fori_loop(kb + 1, NB, lambda qb, cc: unit(qb, cc, False), carry)
        for i in range(NT):
            p = NT * kb + i
            rows = slice(i * T, (i + 1) * T)
            turned = dk[rows] * SCALE
            sig = sig_s[p]
            plain = turned * cos_v[sig] + pltpu.roll(turned, DH // 2, 1) * sin_v[sig]
            dkv_s[p] = jnp.concatenate([plain, dv[rows]], axis=1).astype(BF16)
        return 0

    lax.fori_loop(0, NB - 1, key_block, 0)
    hand_on(0)
    hand_on(1)
    lax.fori_loop(NB - 1, NB, key_block, 0)

    u = x % 2
    pair, other = x + 1 - 2 * u, 3 - x
    pair_dev, other_dev = pair * 4 + y * 2 + q, other * 4 + y * 2 + q

    def k_copy(src, dst, i, k, dev):
        return remote(src, dst, ksem_s.at[i, k], ksem_r.at[i, k], r, dev)

    to_mate = []
    for i, half in enumerate((1 - u, u)):
        for k in range(4):
            e = 4 * half + k
            core_src[i, k] = dkv_s[tags_s[2 * e + (1 - q), 0, 0]]
            to_mate.append(k_copy(core_src.at[i, k], core_buf.at[i, k], i, k, mate))
            to_mate[-1].start()

    def chip_sum(i, k):
        e = 4 * (1 - u if i == 0 else u) + k
        return dkv_s[tags_s[2 * e + q, 0, 0]].astype(F32) + core_buf[i, k].astype(F32)

    to_pair = []
    for k in range(4):
        to_mate[k].wait_recv()
        rs_src[k] = chip_sum(0, k).astype(BF16)
        to_pair.append(k_copy(rs_src.at[k], rs_buf.at[k], 2, k, pair_dev))
        to_pair[-1].start()
    hand_on(2)

    shares, relays = [], []

    def relay(k):
        shares[2 * k].wait_recv()
        relays.append(k_copy(kvbuf.at[pair, k], kvbuf.at[pair, k], 5, k, other_dev))
        relays[-1].start()

    for k in range(4):
        to_mate[4 + k].wait_recv()
        mine = chip_sum(1, k)
        to_pair[k].wait_recv()
        kvbuf[x, k] = (mine + rs_buf[k].astype(F32)).astype(BF16)
        for i, dev in ((3, pair_dev), (4, other_dev)):
            shares.append(k_copy(kvbuf.at[x, k], kvbuf.at[x, k], i, k, dev))
            shares[-1].start()
        if k:
            relay(k - 1)
    relay(3)

    for p in range(N_CP):
        dq_s[p] = (dqt[p // NT, :, (p % NT) * T : (p % NT + 1) * T] * SCALE).T.astype(BF16)
    for m in range(N_CP):
        dq_src[m] = dq_s[place[m]]

    def send_dq(d, _):
        xd, yd, qd, cd = row_peer(d)
        remote(dq_src.at[cd], dq_out.at[:, own], dsem_s, dsem_r, r, cd).start()
        return 0

    lax.fori_loop(1, N_CP, send_dq, 0)
    dq_keep = pltpu.make_async_copy(dq_src.at[c], dq_out.at[:, own], lsem.at[2])
    dq_keep.start()

    keep.wait()
    for send in across:
        send.wait_recv()
    for k in range(4):
        shares[2 * k + 1].wait_recv()
        relays[k].wait_recv()

    w_mates = []

    def tile(start, gg):
        rows = pl.ds(pl.multiple_of(start, 256), 256)
        left, right = (kvbuf[2 * gg + i].reshape(512, 256) for i in range(2))
        return dot(xbuf[0, rows, :], left, 1, 0) + dot(xbuf[1, rows, :], right, 1, 0)

    for yo in range(2):
        for gg in range(2):
            w_src[yo * 256 : (yo + 1) * 256, gg * 256 : (gg + 1) * 256] = tile(
                (1 - q) * 512 + yo * 256, gg
            ).astype(BF16)
        rows = pl.ds(yo * 256, 256)
        w_mate = remote(w_src.at[rows], w_core.at[rows], wsem_s.at[yo], wsem_r.at[yo], r, mate)
        w_mate.start()
        w_mates.append(w_mate)
    for yo in range(2):
        for gg in range(2):
            w_own[yo * 256 : (yo + 1) * 256, gg * 256 : (gg + 1) * 256] = tile(q * 512 + yo * 256, gg)
    for yo in range(2):
        w_mates[yo].wait()
        rows = slice(yo * 256, (yo + 1) * 256)
        block = w_own[rows, :] + w_core[rows, :].astype(F32)
        wsend[:, :, yo] = block.astype(BF16).reshape(8, 2, 16, 512)

    for dz in FAR:
        zd = (z + dz) % 8
        remote(wsend.at[zd], wbuf.at[z], wsem_s.at[2], wsem_r.at[2], zd * 2 + low_y, c).start()
    wbuf[z] = wsend[z]
    take(wbuf.at[pl.ds(0, 7)], wsem_r.at[2])
    for yl in range(2):
        for yo in range(2):
            total = wbuf[0, yl, yo].astype(F32)
            for i in range(1, 8):
                total = total + wbuf[i, yl, yo].astype(F32)
            wsum[yl, yo] = total
    for dl, dy in ((0, 1), (1, 1), (1, 0)):
        yl, yo = (low_y + dl) % 2, (y + dy) % 2
        cd = x * 4 + yo * 2 + q
        remote(wsum.at[yl, yo], wpart.at[2 * low_y + y], wsem_s.at[3], wsem_r.at[3], z * 2 + yl, cd).start()
    wpart[2 * low_y + y] = wsum[low_y, y]
    take(wpart.at[pl.ds(0, 3)], wsem_r.at[3])
    for yy in range(2):
        total = wpart[yy] + wpart[2 + yy]
        for gg in range(2):
            j = 2 * yy + gg
            w_out[:, j * DH : (j + 1) * DH] = total[:, gg * 256 : gg * 256 + DH].astype(BF16)
            w_out[:, 512 + j * DH : 512 + (j + 1) * DH] = total[:, gg * 256 + DH : (gg + 1) * 256].astype(BF16)

    for send in to_mate + to_pair + shares + relays:
        send.wait_send()
    take(dq_src.at[pl.ds(0, N_CP - 1)], dsem_r)
    take(dq_src.at[pl.ds(0, N_CP - 1)], dsem_s)
    dq_keep.wait()
    for i, buf in enumerate((qbuf, kvbuf_in, gbuf, stbuf, tagbuf)):
        take(buf.at[pl.ds(0, N_CP - 1)], asem_s.at[i])
    for send in x_sends + across:
        send.wait_send()
    take(wbuf.at[pl.ds(0, 7)], wsem_s.at[2])
    take(wpart.at[pl.ds(0, 3)], wsem_s.at[3])


def shards(layer_input, queries, keys, values, outputs, out_grad, log_sum_exp, group_first, span_index, seq_length):
    cos_table, sin_table = rope_tables()
    anywhere = pl.BlockSpec(memory_space=pl.ANY)
    vmem = pl.BlockSpec(memory_space=pltpu.VMEM)
    smem = pl.BlockSpec(memory_space=pltpu.SMEM)
    dma = pltpu.SemaphoreType.DMA
    V = pltpu.VMEM
    scratch = [
        V((T, 4096), BF16), V((T, 2048), BF16), V((T, 2048), BF16), V((16, T, DH), F32), V((16, T, DH), F32),
        V((16, T, DH), BF16), V((16, T, DH), BF16), V((16, T, DH), BF16),
        V((16, 8, T), F32), V((16, 8, T), jnp.int32), V((16, 8, T), F32), V((8, T), jnp.int32),
        pltpu.SMEM((16, 8, T), jnp.int32), pltpu.SMEM((16,), jnp.int32),
        V((16, T, DH), BF16), V((16, T, DH), BF16), V((2, 16, T, DH), BF16),
        V((NB, DH, BL), BF16), V((NB, 8, BL), F32), V((NB, DH, BL), F32), V((16, T, 256), BF16),
        V((4, 1024, T), BF16), V((2, 1024, 512), BF16), V((2, 4, T, 256), BF16), V((2, 4, T, 256), BF16),
        V((4, T, 256), BF16), V((4, T, 256), BF16), V((4, 4, T, 256), BF16),
        V((16, T, DH), BF16), V((16, T, DH), BF16), V((512, 512), BF16), V((512, 512), BF16), V((512, 512), F32),
        V((8, 2, 2, 16, 512), BF16), V((8, 2, 2, 16, 512), BF16), V((2, 2, 16, 512), F32), V((4, 16, 512), F32),
        dma((11,)), dma((5,)), dma((5,)), dma((7,)), dma((7,)), dma((6, 4)), dma((6, 4)), dma((4,)), dma((4,)), dma, dma,
    ]
    return pl.pallas_call(
        kernel,
        out_shape=(
            jax.ShapeDtypeStruct((T, 2048), BF16),
            jax.ShapeDtypeStruct((16, 1024), BF16),
        ),
        in_specs=[anywhere] * 6 + [vmem, smem, smem, smem, anywhere, anywhere],
        out_specs=(anywhere, vmem),
        scratch_shapes=scratch,
        compiler_params=pltpu.CompilerParams(
            collective_id=0, has_side_effects=True, vmem_limit_bytes=62 * 1024 * 1024
        ),
        name="attention_backward",
    )(
        layer_input, queries, keys, values, outputs, out_grad, log_sum_exp,
        group_first, span_index, seq_length, jnp.asarray(cos_table), jnp.asarray(sin_table),
    )


def solution(mesh):
    both = P(("dp", "cp"), None)
    placed = (both,) * 7 + (P("dp", "cp"),) * 3
    return jax.shard_map(shards, mesh=mesh, in_specs=placed, out_specs=(both, both), check_vma=False)
```

```python
import math

import jax
import jax.numpy as jnp
import numpy as np
from jax import lax
from jax.experimental import pallas as pl
from jax.experimental.pallas import tpu as pltpu
from jax.sharding import PartitionSpec as P

MESH = pl.DeviceIdType.MESH
F32 = jnp.float32
BF16 = jnp.bfloat16
ROPE_BASE = 500000.0
DH = 128
T = 128
N_CP = 16
N_DP = 16
SCALE = 1.0 / math.sqrt(DH)
LOG2E = math.log2(math.e)
NT = 4
BL = NT * T
NB = N_CP // NT
ORDER = (6, 14, 10, 2, 4, 12, 8, 3, 7, 15, 11, 5, 13, 9, 1)
FAR = (4, 3, 5, 2, 6, 1, 7)


def rope_tables():
    half = DH // 2
    freq = (ROPE_BASE ** (-(np.arange(half) * 2.0 / DH))).astype(np.float32)
    angles = (np.arange(N_CP * T, dtype=np.float32)[:, None] * freq[None, :]).astype(np.float32)
    cosine = np.cos(angles.astype(np.float64))
    sine = np.sin(angles.astype(np.float64))
    cos_table = np.concatenate([cosine, cosine], axis=1).astype(np.float32)
    sin_table = np.concatenate([sine, -sine], axis=1).astype(np.float32)
    return cos_table.reshape(N_CP, T, DH), sin_table.reshape(N_CP, T, DH)


def dot(a, b, ca, cb):
    return lax.dot_general(a, b, (((ca,), (cb,)), ((), ())), preferred_element_type=F32)


def kernel(
    x_hbm, q_hbm, k_hbm, v_hbm, o_hbm, g_hbm, lse_ref, first_ref, span_ref, length_ref, cos_hbm, sin_hbm,
    dq_out, w_out,
    x_v, o_v, g_v, cos_v, sin_v,
    qbuf, gbuf, kvbuf_in, stbuf, tagbuf, st_src, tag_src, tags_s, sig_s,
    qs, gs, kvs, kts, st_s, dqt, dkv_s,
    pbuf, xts, xbuf, core_src, core_buf, pair_src, pair_buf, kvbuf,
    dq_s, dq_src, w_src, w_core, w_own, ysend, ybuf, zsend, zbuf,
    lsem, asem_s, asem_r, xsem_s, xsem_r, ksem_s, ksem_r, wsem_s, wsem_r, dsem_s, dsem_r,
):
    r = lax.axis_index("dp")
    c = lax.axis_index("cp")
    x, y, q = c // 4, (c // 2) % 2, c % 2
    head = 8 * y + 2 * x + q
    mate = x * 4 + y * 2 + (1 - q)

    barrier = pltpu.get_barrier_semaphore()
    z, low_y = r // 2, r % 2
    beside = z * 2 + 1 - low_y
    y_mate = x * 4 + (1 - y) * 2 + q

    def greet(rd, cd):
        pl.semaphore_signal(barrier, inc=1, device_id=(rd, cd), device_id_type=MESH)

    for d in range(1, N_CP):
        greet(r, (c + d) % N_CP)
    for dz in FAR:
        greet(((z + dz) % 8) * 2 + low_y, c)
    greet(beside, c)
    greet(beside, y_mate)

    own = pl.ds(head * DH, DH)
    own_kv = pl.ds((head // 4) * DH, DH)
    kv_hbm = (k_hbm, v_hbm)
    loads = [
        pltpu.make_async_copy(o_hbm, o_v, lsem.at[0]),
        pltpu.make_async_copy(g_hbm, g_v, lsem.at[1]),
        pltpu.make_async_copy(x_hbm, x_v, lsem.at[2]),
        pltpu.make_async_copy(cos_hbm, cos_v, lsem.at[3]),
        pltpu.make_async_copy(sin_hbm, sin_v, lsem.at[4]),
        pltpu.make_async_copy(q_hbm.at[:, own], qbuf.at[c], lsem.at[5]),
        pltpu.make_async_copy(g_hbm.at[:, own], gbuf.at[c], lsem.at[6]),
    ]
    for load in loads:
        load.start()
    for core in range(2):

        @pl.when(q == core)
        def _():
            pltpu.make_async_copy(kv_hbm[core].at[:, own_kv], kvbuf_in.at[c], lsem.at[7]).start()

    pl.semaphore_wait(barrier, (N_CP - 1) + len(FAR) + 2)

    def row_peer(d):
        xd, yd, qd = (x + d // 4) % 4, (y + (d // 2) % 2) % 2, (q + d % 2) % 2
        return xd, yd, qd, xd * 4 + yd * 2 + qd

    def remote(src, dst, send, recv, rd, cd):
        return pltpu.make_async_remote_copy(
            src_ref=src, dst_ref=dst, send_sem=send, recv_sem=recv, device_id=(rd, cd), device_id_type=MESH
        )

    def take(ref, sem):
        pltpu.make_async_copy(ref, ref, sem).wait()

    first = first_ref[0, 0]
    span = span_ref[0, 0]
    length = length_ref[0, 0]
    row_id = lax.broadcasted_iota(jnp.int32, (8, T), 0)
    tag_src[...] = jnp.where(row_id == 0, first + span, jnp.where(row_id == 1, first, 0))
    for d in ORDER:
        xd, yd, qd, cd = row_peer(d)
        kv_cols = pl.ds((2 * yd + xd // 2) * DH, DH)
        for core in range(2):

            @pl.when(qd == core)
            def _():
                remote(kv_hbm[core].at[:, kv_cols], kvbuf_in.at[c], asem_s.at[1], asem_r.at[1], r, cd).start()

        remote(tag_src, tagbuf.at[c], asem_s.at[4], asem_r.at[4], r, cd).start()

    def send_heads(ref, buf, i):
        for d in ORDER:
            xd, yd, qd, cd = row_peer(d)
            cols = pl.ds((8 * yd + 2 * xd + qd) * DH, DH)
            remote(ref.at[:, cols], buf.at[c], asem_s.at[i], asem_r.at[i], r, cd).start()

    send_heads(q_hbm, qbuf, 0)

    pos = span * T + lax.broadcasted_iota(jnp.int32, (1, T), 1)
    low = jnp.where(pos < length, first * T, 2 * N_CP * T).astype(F32)
    lse_t = jnp.concatenate([lse_ref[...] * LOG2E, jnp.zeros((T, T - 16), F32)], axis=1).T
    for load in loads[:2]:
        load.wait()
    lane = lax.broadcasted_iota(jnp.int32, (T, T), 1)
    delta = jnp.zeros((T, T), F32)
    for h in range(16):
        cols = slice(h * DH, (h + 1) * DH)
        part = jnp.sum(o_v[:, cols].astype(F32) * g_v[:, cols].astype(F32), axis=1, keepdims=True)
        delta = jnp.where(lane == h, part, delta)
    delta_t = delta.T
    for h in range(16):
        rows = jnp.concatenate([lse_t[h : h + 1], delta_t[h : h + 1], low, jnp.zeros((5, T), F32)], axis=0)
        st_src[h] = rows

    def send_stats(d, _):
        xd, yd, qd, cd = row_peer(d)
        hd = 8 * yd + 2 * xd + qd
        remote(st_src.at[hd], stbuf.at[c], asem_s.at[3], asem_r.at[3], r, cd).start()
        return 0

    lax.fori_loop(1, N_CP, send_stats, 0)
    send_heads(g_hbm, gbuf, 2)
    stbuf[c] = st_src[head]
    tagbuf[c] = tag_src[...]

    loads[2].wait()

    def turn_x(b, _):
        for part in range(2):
            block = x_v[:, pl.ds(pl.multiple_of(b * 256 + part * 128, 128), 128)].T
            for k in range(8):
                owner = part * 8 + k
                start = (owner % 2) * 512 + (b % 2) * 256 + ((owner // 2) % 2) * 128 + (b // 2) * 16
                xts[owner // 4, pl.ds(pl.multiple_of(start, 16), 16), :] = block[k * 16 : (k + 1) * 16]
        return 0

    lax.fori_loop(0, N_DP, turn_x, 0)

    take(tagbuf.at[pl.ds(0, N_CP - 1)], asem_r.at[4])
    tag_load = pltpu.make_async_copy(tagbuf, tags_s, lsem.at[8])
    tag_load.start()
    tag_load.wait()
    place = [tags_s[m, 0, 0] for m in range(N_CP)]
    member = []
    for p in range(N_CP):
        m = jnp.int32(0)
        for i in range(1, N_CP):
            m = jnp.where(place[i] == p, i, m)
        member.append(m)
        sig_s[p] = p - tags_s[m, 1, 0]

    pltpu.make_async_copy(kvbuf_in.at[c], kvbuf_in.at[c], lsem.at[7]).wait()
    take(kvbuf_in.at[pl.ds(0, N_CP - 1)], asem_r.at[1])
    for p in range(N_CP):
        kvs[q, p] = kvbuf_in[member[p]]
    forward = remote(kvs.at[q], kvs.at[q], lsem.at[9], lsem.at[10], r, mate)
    forward.start()

    for load in loads[3:]:
        load.wait()
    for i, buf in ((0, qbuf), (2, gbuf), (3, stbuf)):
        take(buf.at[pl.ds(0, N_CP - 1)], asem_r.at[i])

    def x_slot(xs, ys):
        return xbuf.at[:, pl.ds(pl.multiple_of((xs * 2 + ys) * T, T), T)]

    x_sends = [
        remote(xts.at[(x + d) % 4], x_slot(x, y), xsem_s.at[i], xsem_r.at[i], r, ((x + d) % 4) * 4 + y * 2 + q)
        for i, d in enumerate((1, 3, 2))
    ]
    x_sends[0].start()
    x_sends[1].start()
    keep = pltpu.make_async_copy(xts.at[x], x_slot(x, y), lsem.at[0])
    keep.start()
    across = [remote(xts.at[x], x_slot(x, y), xsem_s.at[3], xsem_r.at[3], r, y_mate)]
    across[0].start()

    def hand_on(i):
        slot = x_slot((x - (1, 3, 2)[i]) % 4, y)
        x_sends[i].wait_recv()
        across.append(remote(slot, slot, xsem_s.at[4 + i], xsem_r.at[4 + i], r, y_mate))
        across[-1].start()

    for p in range(N_CP):
        qs[p] = qbuf[member[p]]
        gs[p] = gbuf[member[p]]
        st_s[p // NT, :, (p % NT) * T : (p % NT + 1) * T] = stbuf[member[p]]
    forward.wait()
    for p in range(N_CP):
        kts[p // NT, :, (p % NT) * T : (p % NT + 1) * T] = kvs[0, p].T
    dqt[...] = jnp.zeros_like(dqt)

    g, u = x // 2, x % 2
    pair_dev, other_dev = (x + 1 - 2 * u) * 4 + y * 2 + q, (3 - x) * 4 + y * 2 + q
    chunks = [pl.ds(k * 2 * T, 2 * T) for k in range(4)]
    to_mate, to_pair, to_other = {}, {}, {}

    def sum_mate(part):
        for k in range(4):
            for i in range(2):
                e = 2 * k + i
                core_src[part, pl.ds(e * T, T), :] = dkv_s[part, tags_s[2 * e + (1 - q), 0, 0]]
            to_mate[part, k] = remote(
                core_src.at[part, chunks[k]], core_buf.at[part, chunks[k]],
                ksem_s.at[0, part, k], ksem_r.at[0, part, k], r, mate,
            )
            to_mate[part, k].start()

    def chip_sum(part, k):
        own_part = [dkv_s[part, tags_s[2 * (2 * k + i) + q, 0, 0]].astype(F32) for i in range(2)]
        return jnp.concatenate(own_part, axis=0) + core_buf[part, chunks[k], :].astype(F32)

    def sum_pair(part):
        for k in range(4):
            to_mate[part, k].wait_recv()
            pair_src[part, chunks[k], :] = chip_sum(part, k).astype(BF16)
            to_pair[part, k] = remote(
                pair_src.at[part, chunks[k]], pair_buf.at[part, chunks[k]],
                ksem_s.at[1, part, k], ksem_r.at[1, part, k], r, pair_dev,
            )
            to_pair[part, k].start()

    def share(part):
        for k in range(4):
            to_pair[part, k].wait_recv()
            lanes = pl.ds(pl.multiple_of(g * DH, DH), DH)
            total = chip_sum(part, k) + pair_buf[part, chunks[k], :].astype(F32)
            kvbuf[part, chunks[k], lanes] = total.astype(BF16)
            done = kvbuf.at[part, chunks[k], lanes]
            to_other[part, k] = remote(
                done, done, ksem_s.at[2, part, k], ksem_r.at[2, part, k], r, other_dev
            )
            to_other[part, k].start()

    def value_block(step, _):
        kb = NB - 1 - step
        key = kvs[0, pl.ds(NT * kb, NT)].reshape(BL, DH)

        def unit(qb, dv, diagonal):
            query = qs[pl.ds(NT * qb, NT)].reshape(BL, DH)
            grad = gs[pl.ds(NT * qb, NT)].reshape(BL, DH)
            stats = st_s[qb]
            scores = dot(key, query, 1, 1)
            s_at = lax.broadcasted_iota(jnp.int32, (BL, BL), 0)
            allowed = s_at >= stats[2:3].astype(jnp.int32) - kb * BL
            if diagonal:
                allowed = allowed & (s_at <= lax.broadcasted_iota(jnp.int32, (BL, BL), 1))
            probs = jnp.where(allowed, jnp.exp2(scores * (SCALE * LOG2E) - stats[0:1]), 0.0)
            pbuf[kb * NB + qb] = probs
            return dv + dot(probs.astype(BF16), grad, 1, 0)

        dv = unit(kb, jnp.zeros((BL, DH), F32), True)
        dv = lax.fori_loop(kb + 1, NB, lambda qb, t: unit(qb, t, False), dv)
        for i in range(NT):
            dkv_s[0, NT * kb + i] = dv[i * T : (i + 1) * T].astype(BF16)
        return 0

    def key_block(step, _):
        kb = NB - 1 - step
        value = kvs[1, pl.ds(NT * kb, NT)].reshape(BL, DH)
        key_t = kts[kb]

        def unit(qb, dk):
            query = qs[pl.ds(NT * qb, NT)].reshape(BL, DH)
            grad = gs[pl.ds(NT * qb, NT)].reshape(BL, DH)
            dp = dot(value, grad, 1, 1)
            ds = (pbuf[kb * NB + qb] * (dp - st_s[qb][1:2])).astype(BF16)
            dqt[qb] += dot(key_t, ds, 1, 0)
            return dk + dot(ds, query, 1, 0)

        dk = lax.fori_loop(kb, NB, unit, jnp.zeros((BL, DH), F32))
        for i in range(NT):
            p = NT * kb + i
            turned = dk[i * T : (i + 1) * T] * SCALE
            sig = sig_s[p]
            plain = turned * cos_v[sig] + pltpu.roll(turned, DH // 2, 1) * sin_v[sig]
            dkv_s[1, p] = plain.astype(BF16)
        return 0

    lax.fori_loop(0, NB, value_block, 0)
    sum_mate(0)
    x_sends[2].start()
    lax.fori_loop(0, 2, key_block, 0)
    hand_on(0)
    hand_on(1)
    sum_pair(0)
    lax.fori_loop(2, NB, key_block, 0)
    sum_mate(1)
    hand_on(2)
    share(0)
    sum_pair(1)
    share(1)

    for p in range(N_CP):
        dq_s[p] = (dqt[p // NT, :, (p % NT) * T : (p % NT + 1) * T] * SCALE).T.astype(BF16)
    for m in range(N_CP):
        dq_src[m] = dq_s[place[m]]

    def send_dq(d, _):
        xd, yd, qd, cd = row_peer(d)
        remote(dq_src.at[cd], dq_out.at[:, own], dsem_s, dsem_r, r, cd).start()
        return 0

    keep.wait()
    for send in across:
        send.wait_recv()

    def tile(start, part):
        return dot(xbuf[pl.ds(pl.multiple_of(start, 512), 512), :], kvbuf[part], 1, 0).reshape(4, 128, 256)

    def tile_mate(part):
        for k in range(4):
            to_other[part, k].wait_recv()
        w_src[part] = tile((1 - q) * 512, part).astype(BF16)
        w_mates[part] = remote(w_src.at[part], w_core.at[part], wsem_s.at[0, part], wsem_r.at[0, part], r, mate)
        w_mates[part].start()

    def tile_own(part):
        w_own[part] = tile(q * 512, part)

    def send_y(part):
        w_mates[part].wait_recv()
        total = w_own[part] + w_core[part].astype(F32)
        w_own[part] = total
        ysend[part] = total.astype(BF16)
        for dl, dy in ((0, 1), (1, 1), (1, 0)):
            yl, yo = (low_y + dl) % 2, (y + dy) % 2
            remote(
                ysend.at[part, 2 * yl + yo], ybuf.at[part, 2 * low_y + y],
                wsem_s.at[1, part], wsem_r.at[1, part], z * 2 + yl, x * 4 + yo * 2 + q,
            ).start()

    def send_z(part):
        take(ybuf.at[part, pl.ds(0, 3)], wsem_r.at[1, part])
        near = w_own[part, 2 * low_y + y] + ybuf[part, 2 * (1 - low_y) + y].astype(F32)
        far = ybuf[part, 1 - y].astype(F32) + ybuf[part, 3 - y].astype(F32)
        zsend[part, :, y] = near.astype(BF16).reshape(8, 16, 256)
        zsend[part, :, 1 - y] = far.astype(BF16).reshape(8, 16, 256)
        for dz in FAR:
            zd = (z + dz) % 8
            remote(
                zsend.at[part, zd], zbuf.at[part, z], wsem_s.at[2, part], wsem_r.at[2, part], zd * 2 + low_y, c
            ).start()
        zbuf[part, z] = zsend[part, z]

    def finish(part):
        take(zbuf.at[part, pl.ds(0, 7)], wsem_r.at[2, part])
        total = zbuf[part, 0].astype(F32)
        for i in range(1, 8):
            total = total + zbuf[part, i].astype(F32)
        for yy in range(2):
            start = 512 * (1 - part) + 256 * yy
            w_out[:, start : start + 256] = total[yy].astype(BF16)

    w_mates = {}
    tile_mate(0)
    tile_own(0)
    tile_mate(1)
    send_y(0)
    tile_own(1)
    send_y(1)
    send_z(0)
    lax.fori_loop(1, N_CP, send_dq, 0)
    dq_keep = pltpu.make_async_copy(dq_src.at[c], dq_out.at[:, own], lsem.at[2])
    dq_keep.start()
    send_z(1)
    finish(0)
    finish(1)

    for sends in (to_mate, to_pair, to_other):
        for send in sends.values():
            send.wait_send()
    take(dq_src.at[pl.ds(0, N_CP - 1)], dsem_r)
    take(dq_src.at[pl.ds(0, N_CP - 1)], dsem_s)
    dq_keep.wait()
    for i, buf in enumerate((qbuf, kvbuf_in, gbuf, stbuf, tagbuf)):
        take(buf.at[pl.ds(0, N_CP - 1)], asem_s.at[i])
    for send in x_sends + across:
        send.wait_send()
    for part in range(2):
        w_mates[part].wait_send()
        take(ybuf.at[part, pl.ds(0, 3)], wsem_s.at[1, part])
        take(zbuf.at[part, pl.ds(0, 7)], wsem_s.at[2, part])


def shards(layer_input, queries, keys, values, outputs, out_grad, log_sum_exp, group_first, span_index, seq_length):
    cos_table, sin_table = rope_tables()
    anywhere = pl.BlockSpec(memory_space=pl.ANY)
    vmem = pl.BlockSpec(memory_space=pltpu.VMEM)
    smem = pl.BlockSpec(memory_space=pltpu.SMEM)
    dma = pltpu.SemaphoreType.DMA
    V = pltpu.VMEM
    scratch = [
        V((T, 4096), BF16), V((T, 2048), BF16), V((T, 2048), BF16), V((16, T, DH), F32), V((16, T, DH), F32),
        V((16, T, DH), BF16), V((16, T, DH), BF16), V((16, T, DH), BF16),
        V((16, 8, T), F32), V((16, 8, T), jnp.int32), V((16, 8, T), F32), V((8, T), jnp.int32),
        pltpu.SMEM((16, 8, T), jnp.int32), pltpu.SMEM((16,), jnp.int32),
        V((16, T, DH), BF16), V((16, T, DH), BF16), V((2, 16, T, DH), BF16),
        V((NB, DH, BL), BF16), V((NB, 8, BL), F32), V((NB, DH, BL), F32), V((2, 16, T, DH), BF16),
        V((NB * NB, BL, BL), F32), V((4, 1024, T), BF16), V((1024, 1024), BF16), V((2, 1024, DH), BF16),
        V((2, 1024, DH), BF16), V((2, 1024, DH), BF16), V((2, 1024, DH), BF16), V((2, 1024, 256), BF16),
        V((16, T, DH), BF16), V((16, T, DH), BF16), V((2, 4, T, 256), BF16), V((2, 4, T, 256), BF16),
        V((2, 4, T, 256), F32), V((2, 4, T, 256), BF16), V((2, 4, T, 256), BF16),
        V((2, 8, 2, 16, 256), BF16), V((2, 8, 2, 16, 256), BF16),
        dma((11,)), dma((5,)), dma((5,)), dma((7,)), dma((7,)), dma((3, 2, 4)), dma((3, 2, 4)), dma((3, 2)), dma((3, 2)), dma, dma,
    ]
    return pl.pallas_call(
        kernel,
        out_shape=(
            jax.ShapeDtypeStruct((T, 2048), BF16),
            jax.ShapeDtypeStruct((16, 1024), BF16),
        ),
        in_specs=[anywhere] * 6 + [vmem, smem, smem, smem, anywhere, anywhere],
        out_specs=(anywhere, vmem),
        scratch_shapes=scratch,
        compiler_params=pltpu.CompilerParams(
            collective_id=0, has_side_effects=True, vmem_limit_bytes=62 * 1024 * 1024
        ),
        name="attention_backward",
    )(
        layer_input, queries, keys, values, outputs, out_grad, log_sum_exp,
        group_first, span_index, seq_length, jnp.asarray(cos_table), jnp.asarray(sin_table),
    )


def solution(mesh):
    both = P(("dp", "cp"), None)
    placed = (both,) * 7 + (P("dp", "cp"),) * 3
    return jax.shard_map(shards, mesh=mesh, in_specs=placed, out_specs=(both, both), check_vma=False)
```

```python
import math

import jax
import jax.numpy as jnp
import numpy as np
from jax import lax
from jax.experimental import pallas as pl
from jax.experimental.pallas import tpu as pltpu
from jax.sharding import PartitionSpec as P

MESH = pl.DeviceIdType.MESH
F32 = jnp.float32
BF16 = jnp.bfloat16
ROPE_BASE = 500000.0
DH = 128
T = 128
N_CP = 16
N_DP = 16
SCALE = 1.0 / math.sqrt(DH)
LOG2E = math.log2(math.e)
NT = 4
BL = NT * T
NB = N_CP // NT
ORDER = (6, 14, 10, 2, 4, 12, 8, 3, 7, 15, 11, 5, 13, 9, 1)
FAR = (4, 3, 5, 2, 6, 1, 7)


def rope_tables():
    half = DH // 2
    freq = (ROPE_BASE ** (-(np.arange(half) * 2.0 / DH))).astype(np.float32)
    angles = (np.arange(N_CP * T, dtype=np.float32)[:, None] * freq[None, :]).astype(np.float32)
    cosine = np.cos(angles.astype(np.float64))
    sine = np.sin(angles.astype(np.float64))
    cos_table = np.concatenate([cosine, cosine], axis=1).astype(np.float32)
    sin_table = np.concatenate([sine, -sine], axis=1).astype(np.float32)
    return cos_table.reshape(N_CP, T, DH), sin_table.reshape(N_CP, T, DH)


def dot(a, b, ca, cb):
    return lax.dot_general(a, b, (((ca,), (cb,)), ((), ())), preferred_element_type=F32)


def kernel(
    x_hbm, q_hbm, k_hbm, v_hbm, o_hbm, g_hbm, lse_hbm, first_ref, span_ref, length_ref, cos_hbm, sin_hbm,
    dq_out, w_out,
    x_v, o_v, g_v, lse_v, cos_v, sin_v,
    qbuf, gbuf, kvbuf_in, stbuf, tagbuf, st_src, tag_src, tags_s, sig_s,
    qs, gs, kvs, kts, st_s, dqt, dkv_s,
    pbuf, xts, xbuf, core_src, core_buf, pair_src, pair_buf, kvbuf,
    dq_s, dq_src, w_src, w_core, w_own, ysend, ybuf, zsend, zbuf,
    lsem, asem_s, asem_r, xsem_s, xsem_r, ksem_s, ksem_r, wsem_s, wsem_r, dsem_s, dsem_r,
):
    r = lax.axis_index("dp")
    c = lax.axis_index("cp")
    x, y, q = c // 4, (c // 2) % 2, c % 2
    head = 8 * y + 2 * x + q
    mate = x * 4 + y * 2 + (1 - q)

    barrier = pltpu.get_barrier_semaphore()
    z, low_y = r // 2, r % 2
    beside = z * 2 + 1 - low_y
    y_mate = x * 4 + (1 - y) * 2 + q

    def greet(rd, cd):
        pl.semaphore_signal(barrier, inc=1, device_id=(rd, cd), device_id_type=MESH)

    for dz in FAR:
        greet(((z + dz) % 8) * 2 + low_y, c)
    greet(beside, c)
    greet(beside, y_mate)
    for d in range(1, N_CP):
        greet(r, (c + d) % N_CP)

    own = pl.ds(head * DH, DH)
    own_kv = pl.ds((head // 4) * DH, DH)
    kv_hbm = (k_hbm, v_hbm)
    loads = [
        pltpu.make_async_copy(o_hbm, o_v, lsem.at[0]),
        pltpu.make_async_copy(g_hbm, g_v, lsem.at[1]),
        pltpu.make_async_copy(lse_hbm, lse_v, lsem.at[11]),
        pltpu.make_async_copy(x_hbm, x_v, lsem.at[2]),
        pltpu.make_async_copy(cos_hbm, cos_v, lsem.at[3]),
        pltpu.make_async_copy(sin_hbm, sin_v, lsem.at[4]),
        pltpu.make_async_copy(q_hbm.at[:, own], qbuf.at[c], lsem.at[5]),
        pltpu.make_async_copy(g_hbm.at[:, own], gbuf.at[c], lsem.at[6]),
    ]
    for load in loads:
        load.start()
    for core in range(2):

        @pl.when(q == core)
        def _():
            pltpu.make_async_copy(kv_hbm[core].at[:, own_kv], kvbuf_in.at[c], lsem.at[7]).start()

    pl.semaphore_wait(barrier, (N_CP - 1) + len(FAR) + 2)

    def row_peer(d):
        xd, yd, qd = (x + d // 4) % 4, (y + (d // 2) % 2) % 2, (q + d % 2) % 2
        return xd, yd, qd, xd * 4 + yd * 2 + qd

    def remote(src, dst, send, recv, rd, cd):
        return pltpu.make_async_remote_copy(
            src_ref=src, dst_ref=dst, send_sem=send, recv_sem=recv, device_id=(rd, cd), device_id_type=MESH
        )

    def take(ref, sem):
        pltpu.make_async_copy(ref, ref, sem).wait()

    first = first_ref[0, 0]
    span = span_ref[0, 0]
    length = length_ref[0, 0]
    row_id = lax.broadcasted_iota(jnp.int32, (8, T), 0)
    tag_src[...] = jnp.where(row_id == 0, first + span, jnp.where(row_id == 1, first, 0))
    for d in ORDER:
        xd, yd, qd, cd = row_peer(d)
        kv_cols = pl.ds((2 * yd + xd // 2) * DH, DH)
        for core in range(2):

            @pl.when(qd == core)
            def _():
                remote(kv_hbm[core].at[:, kv_cols], kvbuf_in.at[c], asem_s.at[1], asem_r.at[1], r, cd).start()

        remote(tag_src, tagbuf.at[c], asem_s.at[4], asem_r.at[4], r, cd).start()

    def send_heads(ref, buf, i):
        for d in ORDER:
            xd, yd, qd, cd = row_peer(d)
            cols = pl.ds((8 * yd + 2 * xd + qd) * DH, DH)
            remote(ref.at[:, cols], buf.at[c], asem_s.at[i], asem_r.at[i], r, cd).start()

    send_heads(q_hbm, qbuf, 0)

    pos = span * T + lax.broadcasted_iota(jnp.int32, (1, T), 1)
    low = jnp.where(pos < length, first * T, 2 * N_CP * T).astype(F32)
    for load in loads[:3]:
        load.wait()
    lse_t = jnp.concatenate([lse_v[...] * LOG2E, jnp.zeros((T, T - 16), F32)], axis=1).T
    lane = lax.broadcasted_iota(jnp.int32, (T, T), 1)
    delta = jnp.zeros((T, T), F32)
    for h in range(16):
        cols = slice(h * DH, (h + 1) * DH)
        part = jnp.sum(o_v[:, cols].astype(F32) * g_v[:, cols].astype(F32), axis=1, keepdims=True)
        delta = jnp.where(lane == h, part, delta)
    delta_t = delta.T
    for h in range(16):
        rows = jnp.concatenate([lse_t[h : h + 1], delta_t[h : h + 1], low, jnp.zeros((5, T), F32)], axis=0)
        st_src[h] = rows

    def send_stats(d, _):
        xd, yd, qd, cd = row_peer(d)
        hd = 8 * yd + 2 * xd + qd
        remote(st_src.at[hd], stbuf.at[c], asem_s.at[3], asem_r.at[3], r, cd).start()
        return 0

    lax.fori_loop(1, N_CP, send_stats, 0)
    send_heads(g_hbm, gbuf, 2)
    stbuf[c] = st_src[head]
    tagbuf[c] = tag_src[...]

    loads[3].wait()

    def turn_x(b, _):
        for part in range(2):
            block = x_v[:, pl.ds(pl.multiple_of(b * 256 + part * 128, 128), 128)].T
            for k in range(8):
                owner = part * 8 + k
                start = (owner % 2) * 512 + (b % 2) * 256 + ((owner // 2) % 2) * 128 + (b // 2) * 16
                xts[owner // 4, pl.ds(pl.multiple_of(start, 16), 16), :] = block[k * 16 : (k + 1) * 16]
        return 0

    lax.fori_loop(0, N_DP, turn_x, 0)

    take(tagbuf.at[pl.ds(0, N_CP - 1)], asem_r.at[4])
    tag_load = pltpu.make_async_copy(tagbuf, tags_s, lsem.at[8])
    tag_load.start()
    tag_load.wait()
    place = [tags_s[m, 0, 0] for m in range(N_CP)]
    member = []
    for p in range(N_CP):
        m = jnp.int32(0)
        for i in range(1, N_CP):
            m = jnp.where(place[i] == p, i, m)
        member.append(m)
        sig_s[p] = p - tags_s[m, 1, 0]

    pltpu.make_async_copy(kvbuf_in.at[c], kvbuf_in.at[c], lsem.at[7]).wait()
    take(kvbuf_in.at[pl.ds(0, N_CP - 1)], asem_r.at[1])
    for p in range(N_CP):
        kvs[q, p] = kvbuf_in[member[p]]
    forward = remote(kvs.at[q], kvs.at[q], lsem.at[9], lsem.at[10], r, mate)
    forward.start()

    for load in loads[4:7]:
        load.wait()
    take(qbuf.at[pl.ds(0, N_CP - 1)], asem_r.at[0])
    take(stbuf.at[pl.ds(0, N_CP - 1)], asem_r.at[3])
    for p in range(N_CP):
        qs[p] = qbuf[member[p]]
        st_s[p // NT, :, (p % NT) * T : (p % NT + 1) * T] = stbuf[member[p]]
    forward.wait()
    for p in range(N_CP):
        kts[p // NT, :, (p % NT) * T : (p % NT + 1) * T] = kvs[0, p].T
    dqt[...] = jnp.zeros_like(dqt)

    def prob_block(kb, _):
        key = kvs[0, pl.ds(NT * kb, NT)].reshape(BL, DH)

        def unit(qb, diagonal):
            query = qs[pl.ds(NT * qb, NT)].reshape(BL, DH)
            stats = st_s[qb]
            scores = dot(key, query, 1, 1)
            s_at = lax.broadcasted_iota(jnp.int32, (BL, BL), 0)
            allowed = s_at >= stats[2:3].astype(jnp.int32) - kb * BL
            if diagonal:
                allowed = allowed & (s_at <= lax.broadcasted_iota(jnp.int32, (BL, BL), 1))
            pbuf[kb * NB + qb] = jnp.where(allowed, jnp.exp2(scores * (SCALE * LOG2E) - stats[0:1]), 0.0)
            return 0

        unit(kb, True)
        return lax.fori_loop(kb + 1, NB, lambda qb, t: unit(qb, False), 0)

    lax.fori_loop(0, NB, prob_block, 0)
    loads[7].wait()
    take(gbuf.at[pl.ds(0, N_CP - 1)], asem_r.at[2])

    def x_slot(xs, ys):
        return xbuf.at[:, pl.ds(pl.multiple_of((xs * 2 + ys) * T, T), T)]

    x_sends = [
        remote(xts.at[(x + d) % 4], x_slot(x, y), xsem_s.at[i], xsem_r.at[i], r, ((x + d) % 4) * 4 + y * 2 + q)
        for i, d in enumerate((1, 3, 2))
    ]
    for send in x_sends:
        send.start()
    keep = pltpu.make_async_copy(xts.at[x], x_slot(x, y), lsem.at[0])
    keep.start()
    across = [remote(xts.at[x], x_slot(x, y), xsem_s.at[3], xsem_r.at[3], r, y_mate)]
    across[0].start()

    def hand_on(i):
        slot = x_slot((x - (1, 3, 2)[i]) % 4, y)
        x_sends[i].wait_recv()
        across.append(remote(slot, slot, xsem_s.at[4 + i], xsem_r.at[4 + i], r, y_mate))
        across[-1].start()

    for p in range(N_CP):
        gs[p] = gbuf[member[p]]

    g, u = x // 2, x % 2
    pair_dev, other_dev = (x + 1 - 2 * u) * 4 + y * 2 + q, (3 - x) * 4 + y * 2 + q
    chunks = [pl.ds(k * 2 * T, 2 * T) for k in range(4)]
    to_mate, to_pair, to_other = {}, {}, {}

    def sum_mate(part):
        for k in range(4):
            for i in range(2):
                e = 2 * k + i
                core_src[part, pl.ds(e * T, T), :] = dkv_s[part, tags_s[2 * e + (1 - q), 0, 0]]
            to_mate[part, k] = remote(
                core_src.at[part, chunks[k]], core_buf.at[part, chunks[k]],
                ksem_s.at[0, part, k], ksem_r.at[0, part, k], r, mate,
            )
            to_mate[part, k].start()

    def chip_sum(part, k):
        own_part = [dkv_s[part, tags_s[2 * (2 * k + i) + q, 0, 0]].astype(F32) for i in range(2)]
        return jnp.concatenate(own_part, axis=0) + core_buf[part, chunks[k], :].astype(F32)

    def sum_pair(part):
        for k in range(4):
            to_mate[part, k].wait_recv()
            pair_src[part, chunks[k], :] = chip_sum(part, k).astype(BF16)
            to_pair[part, k] = remote(
                pair_src.at[part, chunks[k]], pair_buf.at[part, chunks[k]],
                ksem_s.at[1, part, k], ksem_r.at[1, part, k], r, pair_dev,
            )
            to_pair[part, k].start()

    def share(part):
        for k in range(4):
            to_pair[part, k].wait_recv()
            lanes = pl.ds(pl.multiple_of(g * DH, DH), DH)
            total = chip_sum(part, k) + pair_buf[part, chunks[k], :].astype(F32)
            kvbuf[part, chunks[k], lanes] = total.astype(BF16)
            done = kvbuf.at[part, chunks[k], lanes]
            to_other[part, k] = remote(
                done, done, ksem_s.at[2, part, k], ksem_r.at[2, part, k], r, other_dev
            )
            to_other[part, k].start()

    def value_block(kb, _):
        def unit(qb, dv):
            grad = gs[pl.ds(NT * qb, NT)].reshape(BL, DH)
            return dv + dot(pbuf[kb * NB + qb].astype(BF16), grad, 1, 0)

        dv = lax.fori_loop(kb, NB, unit, jnp.zeros((BL, DH), F32))
        for i in range(NT):
            dkv_s[0, NT * kb + i] = dv[i * T : (i + 1) * T].astype(BF16)
        return 0

    def key_block(step, _):
        kb = NB - 1 - step
        value = kvs[1, pl.ds(NT * kb, NT)].reshape(BL, DH)
        key_t = kts[kb]

        def unit(qb, dk):
            query = qs[pl.ds(NT * qb, NT)].reshape(BL, DH)
            grad = gs[pl.ds(NT * qb, NT)].reshape(BL, DH)
            dp = dot(value, grad, 1, 1)
            ds = (pbuf[kb * NB + qb] * (dp - st_s[qb][1:2])).astype(BF16)
            dqt[qb] += dot(key_t, ds, 1, 0)
            return dk + dot(ds, query, 1, 0)

        dk = lax.fori_loop(kb, NB, unit, jnp.zeros((BL, DH), F32))
        for i in range(NT):
            p = NT * kb + i
            turned = dk[i * T : (i + 1) * T] * SCALE
            sig = sig_s[p]
            plain = turned * cos_v[sig] + pltpu.roll(turned, DH // 2, 1) * sin_v[sig]
            dkv_s[1, p] = plain.astype(BF16)
        return 0

    lax.fori_loop(0, NB, value_block, 0)
    sum_mate(0)
    lax.fori_loop(0, 2, key_block, 0)
    sum_pair(0)
    lax.fori_loop(2, 3, key_block, 0)
    hand_on(0)
    hand_on(1)
    lax.fori_loop(3, NB, key_block, 0)
    sum_mate(1)
    share(0)
    sum_pair(1)
    hand_on(2)
    share(1)

    for p in range(N_CP):
        dq_s[p] = (dqt[p // NT, :, (p % NT) * T : (p % NT + 1) * T] * SCALE).T.astype(BF16)
    for m in range(N_CP):
        dq_src[m] = dq_s[place[m]]

    def send_dq(d, _):
        xd, yd, qd, cd = row_peer(d)
        remote(dq_src.at[cd], dq_out.at[:, own], dsem_s, dsem_r, r, cd).start()
        return 0

    keep.wait()
    for send in across:
        send.wait_recv()

    def tile(start, part):
        return dot(xbuf[pl.ds(pl.multiple_of(start, 512), 512), :], kvbuf[part], 1, 0).reshape(4, 128, 256)

    def tile_mate(part):
        for k in range(4):
            to_other[part, k].wait_recv()
        w_src[part] = tile((1 - q) * 512, part).astype(BF16)
        w_mates[part] = remote(w_src.at[part], w_core.at[part], wsem_s.at[0, part], wsem_r.at[0, part], r, mate)
        w_mates[part].start()

    def tile_own(part):
        w_own[part] = tile(q * 512, part)

    def send_y(part):
        w_mates[part].wait_recv()
        total = w_own[part] + w_core[part].astype(F32)
        w_own[part] = total
        ysend[part] = total.astype(BF16)
        for dl, dy in ((0, 1), (1, 1), (1, 0)):
            yl, yo = (low_y + dl) % 2, (y + dy) % 2
            remote(
                ysend.at[part, 2 * yl + yo], ybuf.at[part, 2 * low_y + y],
                wsem_s.at[1, part], wsem_r.at[1, part], z * 2 + yl, x * 4 + yo * 2 + q,
            ).start()

    def send_z(part):
        take(ybuf.at[part, pl.ds(0, 3)], wsem_r.at[1, part])
        near = w_own[part, 2 * low_y + y] + ybuf[part, 2 * (1 - low_y) + y].astype(F32)
        far = ybuf[part, 1 - y].astype(F32) + ybuf[part, 3 - y].astype(F32)
        zsend[part, :, y] = near.astype(BF16).reshape(8, 16, 256)
        zsend[part, :, 1 - y] = far.astype(BF16).reshape(8, 16, 256)
        for dz in FAR:
            zd = (z + dz) % 8
            remote(
                zsend.at[part, zd], zbuf.at[part, z], wsem_s.at[2, part], wsem_r.at[2, part], zd * 2 + low_y, c
            ).start()
        zbuf[part, z] = zsend[part, z]

    def finish(part):
        take(zbuf.at[part, pl.ds(0, 7)], wsem_r.at[2, part])
        total = zbuf[part, 0].astype(F32)
        for i in range(1, 8):
            total = total + zbuf[part, i].astype(F32)
        for yy in range(2):
            start = 512 * (1 - part) + 256 * yy
            w_out[:, start : start + 256] = total[yy].astype(BF16)

    w_mates = {}
    tile_mate(0)
    tile_own(0)
    tile_mate(1)
    send_y(0)
    tile_own(1)
    send_y(1)
    send_z(0)
    lax.fori_loop(1, N_CP, send_dq, 0)
    dq_keep = pltpu.make_async_copy(dq_src.at[c], dq_out.at[:, own], lsem.at[2])
    dq_keep.start()
    send_z(1)
    finish(0)
    finish(1)

    for sends in (to_mate, to_pair, to_other):
        for send in sends.values():
            send.wait_send()
    take(dq_src.at[pl.ds(0, N_CP - 1)], dsem_r)
    take(dq_src.at[pl.ds(0, N_CP - 1)], dsem_s)
    dq_keep.wait()
    for i, buf in enumerate((qbuf, kvbuf_in, gbuf, stbuf, tagbuf)):
        take(buf.at[pl.ds(0, N_CP - 1)], asem_s.at[i])
    for send in x_sends + across:
        send.wait_send()
    for part in range(2):
        w_mates[part].wait_send()
        take(ybuf.at[part, pl.ds(0, 3)], wsem_s.at[1, part])
        take(zbuf.at[part, pl.ds(0, 7)], wsem_s.at[2, part])


def shards(layer_input, queries, keys, values, outputs, out_grad, log_sum_exp, group_first, span_index, seq_length):
    cos_table, sin_table = rope_tables()
    anywhere = pl.BlockSpec(memory_space=pl.ANY)
    vmem = pl.BlockSpec(memory_space=pltpu.VMEM)
    smem = pl.BlockSpec(memory_space=pltpu.SMEM)
    dma = pltpu.SemaphoreType.DMA
    V = pltpu.VMEM
    scratch = [
        V((T, 4096), BF16), V((T, 2048), BF16), V((T, 2048), BF16), V((T, 16), F32), V((16, T, DH), F32), V((16, T, DH), F32),
        V((16, T, DH), BF16), V((16, T, DH), BF16), V((16, T, DH), BF16),
        V((16, 8, T), F32), V((16, 8, T), jnp.int32), V((16, 8, T), F32), V((8, T), jnp.int32),
        pltpu.SMEM((16, 8, T), jnp.int32), pltpu.SMEM((16,), jnp.int32),
        V((16, T, DH), BF16), V((16, T, DH), BF16), V((2, 16, T, DH), BF16),
        V((NB, DH, BL), BF16), V((NB, 8, BL), F32), V((NB, DH, BL), F32), V((2, 16, T, DH), BF16),
        V((NB * NB, BL, BL), F32), V((4, 1024, T), BF16), V((1024, 1024), BF16), V((2, 1024, DH), BF16),
        V((2, 1024, DH), BF16), V((2, 1024, DH), BF16), V((2, 1024, DH), BF16), V((2, 1024, 256), BF16),
        V((16, T, DH), BF16), V((16, T, DH), BF16), V((2, 4, T, 256), BF16), V((2, 4, T, 256), BF16),
        V((2, 4, T, 256), F32), V((2, 4, T, 256), BF16), V((2, 4, T, 256), BF16),
        V((2, 8, 2, 16, 256), BF16), V((2, 8, 2, 16, 256), BF16),
        dma((12,)), dma((5,)), dma((5,)), dma((7,)), dma((7,)), dma((3, 2, 4)), dma((3, 2, 4)), dma((3, 2)), dma((3, 2)), dma, dma,
    ]
    return pl.pallas_call(
        kernel,
        out_shape=(
            jax.ShapeDtypeStruct((T, 2048), BF16),
            jax.ShapeDtypeStruct((16, 1024), BF16),
        ),
        in_specs=[anywhere] * 7 + [smem, smem, smem, anywhere, anywhere],
        out_specs=(anywhere, vmem),
        scratch_shapes=scratch,
        compiler_params=pltpu.CompilerParams(
            collective_id=0, has_side_effects=True, vmem_limit_bytes=62 * 1024 * 1024
        ),
        name="attention_backward",
    )(
        layer_input, queries, keys, values, outputs, out_grad, log_sum_exp,
        group_first, span_index, seq_length, jnp.asarray(cos_table), jnp.asarray(sin_table),
    )


def solution(mesh):
    both = P(("dp", "cp"), None)
    placed = (both,) * 7 + (P("dp", "cp"),) * 3
    return jax.shard_map(shards, mesh=mesh, in_specs=placed, out_specs=(both, both), check_vma=False)
```

```python
import math

import jax
import jax.numpy as jnp
import numpy as np
from jax import lax
from jax.experimental import pallas as pl
from jax.experimental.pallas import tpu as pltpu
from jax.sharding import PartitionSpec as P

MESH = pl.DeviceIdType.MESH
F32 = jnp.float32
BF16 = jnp.bfloat16
ROPE_BASE = 500000.0
DH = 128
T = 128
N_CP = 16
N_DP = 16
SCALE = 1.0 / math.sqrt(DH)
LOG2E = math.log2(math.e)
NT = 4
BL = NT * T
NB = N_CP // NT
ORDER = (6, 14, 10, 2, 4, 12, 8, 3, 7, 15, 11, 5, 13, 9, 1)
HOME = ((6, 14, 10, 2, 7, 15, 11, 3), (4, 12, 8, 5, 13, 9, 1))
FAR = (4, 3, 5, 2, 6, 1, 7)


def rope_tables():
    half = DH // 2
    freq = (ROPE_BASE ** (-(np.arange(half) * 2.0 / DH))).astype(np.float32)
    angles = (np.arange(N_CP * T, dtype=np.float32)[:, None] * freq[None, :]).astype(np.float32)
    cosine = np.cos(angles.astype(np.float64))
    sine = np.sin(angles.astype(np.float64))
    cos_table = np.concatenate([cosine, cosine], axis=1).astype(np.float32)
    sin_table = np.concatenate([sine, -sine], axis=1).astype(np.float32)
    return cos_table.reshape(N_CP, T, DH), sin_table.reshape(N_CP, T, DH)


def dot(a, b, ca, cb):
    return lax.dot_general(a, b, (((ca,), (cb,)), ((), ())), preferred_element_type=F32)


def kernel(
    x_hbm, q_hbm, k_hbm, v_hbm, o_hbm, g_hbm, lse_hbm, first_ref, span_ref, length_ref, cos_hbm, sin_hbm,
    dq_out, w_out,
    x_v, o_v, g_v, lse_v, cos_v, sin_v,
    qbuf, gbuf, kvbuf_in, stbuf, tagbuf, st_src, tag_src, tags_s, sig_s,
    qs, gs, kvs, kts, st_s, dqt, dkv_s,
    pbuf, xts, xbuf, core_src, core_buf, pair_src, pair_buf, kvbuf,
    dq_s, dq_src, w_src, w_core, w_own, w_sum, ysend, ybuf, zsend, zbuf,
    lsem, asem_s, asem_r, xsem_s, xsem_r, ksem_s, ksem_r, wsem_s, wsem_r, dsem_s, dsem_r, ysem_s, ysem_r, zsem_s, zsem_r,
):
    r = lax.axis_index("dp")
    c = lax.axis_index("cp")
    x, y, q = c // 4, (c // 2) % 2, c % 2
    head = 8 * y + 2 * x + q
    mate = x * 4 + y * 2 + (1 - q)

    barrier = pltpu.get_barrier_semaphore()
    z, low_y = r // 2, r % 2
    beside = z * 2 + 1 - low_y
    y_mate = x * 4 + (1 - y) * 2 + q

    def greet(rd, cd):
        pl.semaphore_signal(barrier, inc=1, device_id=(rd, cd), device_id_type=MESH)

    for dz in FAR:
        greet(((z + dz) % 8) * 2 + low_y, c)
    greet(beside, c)
    greet(beside, y_mate)
    for d in range(1, N_CP):
        greet(r, (c + d) % N_CP)

    own = pl.ds(head * DH, DH)
    own_kv = pl.ds((head // 4) * DH, DH)
    kv_hbm = (k_hbm, v_hbm)
    loads = [
        pltpu.make_async_copy(o_hbm, o_v, lsem.at[0]),
        pltpu.make_async_copy(g_hbm, g_v, lsem.at[1]),
        pltpu.make_async_copy(lse_hbm, lse_v, lsem.at[11]),
        pltpu.make_async_copy(x_hbm, x_v, lsem.at[2]),
        pltpu.make_async_copy(cos_hbm, cos_v, lsem.at[3]),
        pltpu.make_async_copy(sin_hbm, sin_v, lsem.at[4]),
        pltpu.make_async_copy(q_hbm.at[:, own], qbuf.at[c], lsem.at[5]),
        pltpu.make_async_copy(g_hbm.at[:, own], gbuf.at[c], lsem.at[6]),
    ]
    for load in loads:
        load.start()
    for core in range(2):

        @pl.when(q == core)
        def _():
            pltpu.make_async_copy(kv_hbm[core].at[:, own_kv], kvbuf_in.at[c], lsem.at[7]).start()

    pl.semaphore_wait(barrier, (N_CP - 1) + len(FAR) + 2)

    def row_peer(d):
        xd, yd, qd = (x + d // 4) % 4, (y + (d // 2) % 2) % 2, (q + d % 2) % 2
        return xd, yd, qd, xd * 4 + yd * 2 + qd

    def remote(src, dst, send, recv, rd, cd):
        return pltpu.make_async_remote_copy(
            src_ref=src, dst_ref=dst, send_sem=send, recv_sem=recv, device_id=(rd, cd), device_id_type=MESH
        )

    def take(ref, sem):
        pltpu.make_async_copy(ref, ref, sem).wait()

    first = first_ref[0, 0]
    span = span_ref[0, 0]
    length = length_ref[0, 0]
    row_id = lax.broadcasted_iota(jnp.int32, (8, T), 0)
    tag_src[...] = jnp.where(row_id == 0, first + span, jnp.where(row_id == 1, first, 0))
    for d in ORDER:
        xd, yd, qd, cd = row_peer(d)
        kv_cols = pl.ds((2 * yd + xd // 2) * DH, DH)
        for core in range(2):

            @pl.when(qd == core)
            def _():
                remote(kv_hbm[core].at[:, kv_cols], kvbuf_in.at[c], asem_s.at[1], asem_r.at[1], r, cd).start()

        remote(tag_src, tagbuf.at[c], asem_s.at[4], asem_r.at[4], r, cd).start()

    def send_heads(ref, buf, i):
        for d in ORDER:
            xd, yd, qd, cd = row_peer(d)
            cols = pl.ds((8 * yd + 2 * xd + qd) * DH, DH)
            remote(ref.at[:, cols], buf.at[c], asem_s.at[i], asem_r.at[i], r, cd).start()

    send_heads(q_hbm, qbuf, 0)

    pos = span * T + lax.broadcasted_iota(jnp.int32, (1, T), 1)
    low = jnp.where(pos < length, first * T, 2 * N_CP * T).astype(F32)
    for load in loads[:3]:
        load.wait()
    lse_t = jnp.concatenate([lse_v[...] * LOG2E, jnp.zeros((T, T - 16), F32)], axis=1).T
    lane = lax.broadcasted_iota(jnp.int32, (T, T), 1)
    delta = jnp.zeros((T, T), F32)
    for h in range(16):
        cols = slice(h * DH, (h + 1) * DH)
        part = jnp.sum(o_v[:, cols].astype(F32) * g_v[:, cols].astype(F32), axis=1, keepdims=True)
        delta = jnp.where(lane == h, part, delta)
    delta_t = delta.T
    for h in range(16):
        rows = jnp.concatenate([lse_t[h : h + 1], delta_t[h : h + 1], low, jnp.zeros((5, T), F32)], axis=0)
        st_src[h] = rows

    def send_stats(d, _):
        xd, yd, qd, cd = row_peer(d)
        hd = 8 * yd + 2 * xd + qd
        remote(st_src.at[hd], stbuf.at[c], asem_s.at[3], asem_r.at[3], r, cd).start()
        return 0

    lax.fori_loop(1, N_CP, send_stats, 0)
    send_heads(g_hbm, gbuf, 2)
    stbuf[c] = st_src[head]
    tagbuf[c] = tag_src[...]

    loads[3].wait()

    def turn_x(b, _):
        for part in range(2):
            block = x_v[:, pl.ds(pl.multiple_of(b * 256 + part * 128, 128), 128)].T
            for k in range(8):
                owner = part * 8 + k
                start = (owner % 2) * 512 + (b % 2) * 256 + ((owner // 2) % 2) * 128 + (b // 2) * 16
                xts[owner // 4, pl.ds(pl.multiple_of(start, 16), 16), :] = block[k * 16 : (k + 1) * 16]
        return 0

    lax.fori_loop(0, N_DP, turn_x, 0)

    take(tagbuf.at[pl.ds(0, N_CP - 1)], asem_r.at[4])
    tag_load = pltpu.make_async_copy(tagbuf, tags_s, lsem.at[8])
    tag_load.start()
    tag_load.wait()
    place = [tags_s[m, 0, 0] for m in range(N_CP)]
    member = []
    for p in range(N_CP):
        m = jnp.int32(0)
        for i in range(1, N_CP):
            m = jnp.where(place[i] == p, i, m)
        member.append(m)
        sig_s[p] = p - tags_s[m, 1, 0]

    pltpu.make_async_copy(kvbuf_in.at[c], kvbuf_in.at[c], lsem.at[7]).wait()
    take(kvbuf_in.at[pl.ds(0, N_CP - 1)], asem_r.at[1])
    for p in range(N_CP):
        kvs[q, p] = kvbuf_in[member[p]]
    forward = remote(kvs.at[q], kvs.at[q], lsem.at[9], lsem.at[10], r, mate)
    forward.start()

    for load in loads[4:7]:
        load.wait()
    take(qbuf.at[pl.ds(0, N_CP - 1)], asem_r.at[0])
    take(stbuf.at[pl.ds(0, N_CP - 1)], asem_r.at[3])
    for p in range(N_CP):
        qs[p] = qbuf[member[p]]
        st_s[p // NT, :, (p % NT) * T : (p % NT + 1) * T] = stbuf[member[p]]
    forward.wait()
    for p in range(N_CP):
        kts[p // NT, :, (p % NT) * T : (p % NT + 1) * T] = kvs[0, p].T
    dqt[...] = jnp.zeros_like(dqt)

    def prob_block(kb, _):
        key = kvs[0, pl.ds(NT * kb, NT)].reshape(BL, DH)

        def unit(qb, diagonal):
            query = qs[pl.ds(NT * qb, NT)].reshape(BL, DH)
            stats = st_s[qb]
            scores = dot(key, query, 1, 1)
            s_at = lax.broadcasted_iota(jnp.int32, (BL, BL), 0)
            allowed = s_at >= stats[2:3].astype(jnp.int32) - kb * BL
            if diagonal:
                allowed = allowed & (s_at <= lax.broadcasted_iota(jnp.int32, (BL, BL), 1))
            pbuf[kb * NB + qb] = jnp.where(allowed, jnp.exp2(scores * (SCALE * LOG2E) - stats[0:1]), 0.0)
            return 0

        unit(kb, True)
        return lax.fori_loop(kb + 1, NB, lambda qb, t: unit(qb, False), 0)

    lax.fori_loop(0, NB, prob_block, 0)
    loads[7].wait()
    take(gbuf.at[pl.ds(0, N_CP - 1)], asem_r.at[2])

    def x_slot(xs, ys):
        return xbuf.at[:, pl.ds(pl.multiple_of((xs * 2 + ys) * T, T), T)]

    x_sends = [
        remote(xts.at[(x + d) % 4], x_slot(x, y), xsem_s.at[i], xsem_r.at[i], r, ((x + d) % 4) * 4 + y * 2 + q)
        for i, d in enumerate((1, 3, 2))
    ]
    for send in x_sends:
        send.start()
    keep = pltpu.make_async_copy(xts.at[x], x_slot(x, y), lsem.at[0])
    keep.start()
    across = [remote(xts.at[x], x_slot(x, y), xsem_s.at[3], xsem_r.at[3], r, y_mate)]
    across[0].start()

    def hand_on(i):
        slot = x_slot((x - (1, 3, 2)[i]) % 4, y)
        x_sends[i].wait_recv()
        across.append(remote(slot, slot, xsem_s.at[4 + i], xsem_r.at[4 + i], r, y_mate))
        across[-1].start()

    for p in range(N_CP):
        gs[p] = gbuf[member[p]]

    g, u = x // 2, x % 2
    pair_dev, other_dev = (x + 1 - 2 * u) * 4 + y * 2 + q, (3 - x) * 4 + y * 2 + q
    chunks = [pl.ds(k * 2 * T, 2 * T) for k in range(4)]
    to_mate, to_pair, to_other = {}, {}, {}

    def sum_mate(part):
        for k in range(4):
            for i in range(2):
                e = 2 * k + i
                core_src[part, pl.ds(e * T, T), :] = dkv_s[part, tags_s[2 * e + (1 - q), 0, 0]]
            to_mate[part, k] = remote(
                core_src.at[part, chunks[k]], core_buf.at[part, chunks[k]],
                ksem_s.at[0, part, k], ksem_r.at[0, part, k], r, mate,
            )
            to_mate[part, k].start()

    def chip_sum(part, k):
        own_part = [dkv_s[part, tags_s[2 * (2 * k + i) + q, 0, 0]].astype(F32) for i in range(2)]
        return jnp.concatenate(own_part, axis=0) + core_buf[part, chunks[k], :].astype(F32)

    def sum_pair(part):
        for k in range(4):
            to_mate[part, k].wait_recv()
            pair_src[part, chunks[k], :] = chip_sum(part, k).astype(BF16)
            to_pair[part, k] = remote(
                pair_src.at[part, chunks[k]], pair_buf.at[part, chunks[k]],
                ksem_s.at[1, part, k], ksem_r.at[1, part, k], r, pair_dev,
            )
            to_pair[part, k].start()

    def share(part):
        for k in range(4):
            to_pair[part, k].wait_recv()
            lanes = pl.ds(pl.multiple_of(g * DH, DH), DH)
            total = chip_sum(part, k) + pair_buf[part, chunks[k], :].astype(F32)
            kvbuf[part, chunks[k], lanes] = total.astype(BF16)
            done = kvbuf.at[part, chunks[k], lanes]
            to_other[part, k] = remote(
                done, done, ksem_s.at[2, part, k], ksem_r.at[2, part, k], r, other_dev
            )
            to_other[part, k].start()

    def value_block(kb, _):
        def unit(qb, dv):
            grad = gs[pl.ds(NT * qb, NT)].reshape(BL, DH)
            return dv + dot(pbuf[kb * NB + qb].astype(BF16), grad, 1, 0)

        dv = lax.fori_loop(kb, NB, unit, jnp.zeros((BL, DH), F32))
        for i in range(NT):
            dkv_s[0, NT * kb + i] = dv[i * T : (i + 1) * T].astype(BF16)
        return 0

    def key_block(step, _):
        kb = NB - 1 - step
        value = kvs[1, pl.ds(NT * kb, NT)].reshape(BL, DH)
        key_t = kts[kb]

        def unit(qb, dk):
            query = qs[pl.ds(NT * qb, NT)].reshape(BL, DH)
            grad = gs[pl.ds(NT * qb, NT)].reshape(BL, DH)
            dp = dot(value, grad, 1, 1)
            ds = (pbuf[kb * NB + qb] * (dp - st_s[qb][1:2])).astype(BF16)
            dqt[qb] += dot(key_t, ds, 1, 0)
            return dk + dot(ds, query, 1, 0)

        dk = lax.fori_loop(kb, NB, unit, jnp.zeros((BL, DH), F32))
        for i in range(NT):
            p = NT * kb + i
            turned = dk[i * T : (i + 1) * T] * SCALE
            sig = sig_s[p]
            plain = turned * cos_v[sig] + pltpu.roll(turned, DH // 2, 1) * sin_v[sig]
            dkv_s[1, p] = plain.astype(BF16)
        return 0

    lax.fori_loop(0, NB, value_block, 0)
    sum_mate(0)
    lax.fori_loop(0, 2, key_block, 0)
    sum_pair(0)
    lax.fori_loop(2, 3, key_block, 0)
    hand_on(0)
    hand_on(1)
    lax.fori_loop(3, NB, key_block, 0)
    sum_mate(1)
    share(0)
    sum_pair(1)
    hand_on(2)
    share(1)

    for p in range(N_CP):
        dq_s[p] = (dqt[p // NT, :, (p % NT) * T : (p % NT + 1) * T] * SCALE).T.astype(BF16)
    for m in range(N_CP):
        dq_src[m] = dq_s[place[m]]

    def send_dq(d, _):
        xd, yd, qd, cd = row_peer(d)
        remote(dq_src.at[cd], dq_out.at[:, own], dsem_s, dsem_r, r, cd).start()
        return 0

    keep.wait()
    for send in across:
        send.wait_recv()

    def tile(start, part):
        return dot(xbuf[pl.ds(pl.multiple_of(start, 512), 512), :], kvbuf[part], 1, 0).reshape(4, 128, 256)

    def tile_mate(part):
        for k in range(4):
            to_other[part, k].wait_recv()
        w_src[part] = tile((1 - q) * 512, part).astype(BF16)
        w_mates[part] = remote(w_src.at[part], w_core.at[part], wsem_s.at[part], wsem_r.at[part], r, mate)
        w_mates[part].start()

    def tile_own(part):
        w_own[part] = tile(q * 512, part)

    def send_y(part, half):
        cols = slice(half * DH, (half + 1) * DH)
        if half == 0:
            w_mates[part].wait_recv()
        total = w_own[part, :, :, cols] + w_core[part, :, :, cols].astype(F32)
        j = 2 * part + half
        w_sum[j] = total
        ysend[j] = total.astype(BF16)
        for dl, dy in ((0, 1), (1, 1), (1, 0)):
            yl, yo = (low_y + dl) % 2, (y + dy) % 2
            remote(
                ysend.at[j, 2 * yl + yo], ybuf.at[j, 2 * low_y + y],
                ysem_s.at[j], ysem_r.at[j], z * 2 + yl, x * 4 + yo * 2 + q,
            ).start()

    def send_z(j):
        take(ybuf.at[j, pl.ds(0, 3)], ysem_r.at[j])
        near = w_sum[j, 2 * low_y + y] + ybuf[j, 2 * (1 - low_y) + y].astype(F32)
        far = ybuf[j, 1 - y].astype(F32) + ybuf[j, 3 - y].astype(F32)
        zsend[j, :, y] = near.astype(BF16).reshape(8, 16, DH)
        zsend[j, :, 1 - y] = far.astype(BF16).reshape(8, 16, DH)
        for dz in FAR:
            zd = (z + dz) % 8
            remote(zsend.at[j, zd], zbuf.at[j, z], zsem_s.at[j], zsem_r.at[j], zd * 2 + low_y, c).start()
        zbuf[j, z] = zsend[j, z]

    def finish(j):
        take(zbuf.at[j, pl.ds(0, 7)], zsem_r.at[j])
        total = zbuf[j, 0].astype(F32)
        for i in range(1, 8):
            total = total + zbuf[j, i].astype(F32)
        for yy in range(2):
            start = 512 * (1 - j // 2) + 256 * yy + DH * (j % 2)
            w_out[:, start : start + DH] = total[yy].astype(BF16)

    w_mates = {}
    for d in HOME[0]:
        send_dq(d, 0)
    tile_mate(0)
    tile_own(0)
    tile_mate(1)
    send_y(0, 0)
    send_y(0, 1)
    tile_own(1)
    send_y(1, 0)
    send_y(1, 1)
    send_z(0)
    for d in HOME[1]:
        send_dq(d, 0)
    dq_keep = pltpu.make_async_copy(dq_src.at[c], dq_out.at[:, own], lsem.at[2])
    dq_keep.start()
    send_z(1)
    send_z(2)
    send_z(3)
    for j in range(4):
        finish(j)

    for sends in (to_mate, to_pair, to_other):
        for send in sends.values():
            send.wait_send()
    take(dq_src.at[pl.ds(0, N_CP - 1)], dsem_r)
    take(dq_src.at[pl.ds(0, N_CP - 1)], dsem_s)
    dq_keep.wait()
    for i, buf in enumerate((qbuf, kvbuf_in, gbuf, stbuf, tagbuf)):
        take(buf.at[pl.ds(0, N_CP - 1)], asem_s.at[i])
    for send in x_sends + across:
        send.wait_send()
    for part in range(2):
        w_mates[part].wait_send()
    for j in range(4):
        take(ybuf.at[j, pl.ds(0, 3)], ysem_s.at[j])
        take(zbuf.at[j, pl.ds(0, 7)], zsem_s.at[j])


def shards(layer_input, queries, keys, values, outputs, out_grad, log_sum_exp, group_first, span_index, seq_length):
    cos_table, sin_table = rope_tables()
    anywhere = pl.BlockSpec(memory_space=pl.ANY)
    vmem = pl.BlockSpec(memory_space=pltpu.VMEM)
    smem = pl.BlockSpec(memory_space=pltpu.SMEM)
    dma = pltpu.SemaphoreType.DMA
    V = pltpu.VMEM
    scratch = [
        V((T, 4096), BF16), V((T, 2048), BF16), V((T, 2048), BF16), V((T, 16), F32), V((16, T, DH), F32), V((16, T, DH), F32),
        V((16, T, DH), BF16), V((16, T, DH), BF16), V((16, T, DH), BF16),
        V((16, 8, T), F32), V((16, 8, T), jnp.int32), V((16, 8, T), F32), V((8, T), jnp.int32),
        pltpu.SMEM((16, 8, T), jnp.int32), pltpu.SMEM((16,), jnp.int32),
        V((16, T, DH), BF16), V((16, T, DH), BF16), V((2, 16, T, DH), BF16),
        V((NB, DH, BL), BF16), V((NB, 8, BL), F32), V((NB, DH, BL), F32), V((2, 16, T, DH), BF16),
        V((NB * NB, BL, BL), F32), V((4, 1024, T), BF16), V((1024, 1024), BF16), V((2, 1024, DH), BF16),
        V((2, 1024, DH), BF16), V((2, 1024, DH), BF16), V((2, 1024, DH), BF16), V((2, 1024, 256), BF16),
        V((16, T, DH), BF16), V((16, T, DH), BF16), V((2, 4, T, 256), BF16), V((2, 4, T, 256), BF16),
        V((2, 4, T, 256), F32), V((4, 4, T, DH), F32), V((4, 4, T, DH), BF16), V((4, 4, T, DH), BF16),
        V((4, 8, 2, 16, DH), BF16), V((4, 8, 2, 16, DH), BF16),
        dma((12,)), dma((5,)), dma((5,)), dma((7,)), dma((7,)), dma((3, 2, 4)), dma((3, 2, 4)), dma((2,)), dma((2,)), dma, dma,
        dma((4,)), dma((4,)), dma((4,)), dma((4,)),
    ]
    return pl.pallas_call(
        kernel,
        out_shape=(
            jax.ShapeDtypeStruct((T, 2048), BF16),
            jax.ShapeDtypeStruct((16, 1024), BF16),
        ),
        in_specs=[anywhere] * 7 + [smem, smem, smem, anywhere, anywhere],
        out_specs=(anywhere, vmem),
        scratch_shapes=scratch,
        compiler_params=pltpu.CompilerParams(
            collective_id=0, has_side_effects=True, vmem_limit_bytes=62 * 1024 * 1024
        ),
        name="attention_backward",
    )(
        layer_input, queries, keys, values, outputs, out_grad, log_sum_exp,
        group_first, span_index, seq_length, jnp.asarray(cos_table), jnp.asarray(sin_table),
    )


def solution(mesh):
    both = P(("dp", "cp"), None)
    placed = (both,) * 7 + (P("dp", "cp"),) * 3
    return jax.shard_map(shards, mesh=mesh, in_specs=placed, out_specs=(both, both), check_vma=False)
```

```python
import math

import jax
import jax.numpy as jnp
import numpy as np
from jax import lax
from jax.experimental import pallas as pl
from jax.experimental.pallas import tpu as pltpu
from jax.sharding import PartitionSpec as P

MESH = pl.DeviceIdType.MESH
F32 = jnp.float32
BF16 = jnp.bfloat16
ROPE_BASE = 500000.0
DH = 128
T = 128
N_CP = 16
N_DP = 16
SCALE = 1.0 / math.sqrt(DH)
LOG2E = math.log2(math.e)
NT = 4
BL = NT * T
NB = N_CP // NT
ORDER = (6, 14, 10, 2, 4, 12, 8, 3, 7, 15, 11, 5, 13, 9, 1)
HOME = ((6, 14, 10, 2, 7, 15, 11, 3), (4, 12, 8, 5, 13, 9, 1))
FAR = (4, 3, 5, 2, 6, 1, 7)


def rope_tables():
    half = DH // 2
    freq = (ROPE_BASE ** (-(np.arange(half) * 2.0 / DH))).astype(np.float32)
    angles = (np.arange(N_CP * T, dtype=np.float32)[:, None] * freq[None, :]).astype(np.float32)
    cosine = np.cos(angles.astype(np.float64))
    sine = np.sin(angles.astype(np.float64))
    cos_table = np.concatenate([cosine, cosine], axis=1).astype(np.float32)
    sin_table = np.concatenate([sine, -sine], axis=1).astype(np.float32)
    return cos_table.reshape(N_CP, T, DH), sin_table.reshape(N_CP, T, DH)


def dot(a, b, ca, cb):
    return lax.dot_general(a, b, (((ca,), (cb,)), ((), ())), preferred_element_type=F32)


def kernel(
    x_hbm, q_hbm, k_hbm, v_hbm, o_hbm, g_hbm, lse_hbm, first_ref, span_ref, length_ref, cos_hbm, sin_hbm,
    dq_out, w_out,
    x_v, o_v, g_v, lse_v, cos_v, sin_v,
    qbuf, gbuf, kvbuf_in, stbuf, tagbuf, st_src, tag_src, tags_s, sig_s,
    qs, gs, kvs, kts, st_s, dqt, dkv_s,
    pbuf, xts, xbuf, core_src, core_buf, pair_src, pair_buf, kvbuf,
    dq_s, dq_src, w_src, w_core, w_own, w_sum, ysend, ybuf, zsend, zbuf,
    lsem, asem_s, asem_r, xsem_s, xsem_r, ksem_s, ksem_r, wsem_s, wsem_r, dsem_s, dsem_r, ysem_s, ysem_r, zsem_s, zsem_r,
):
    r = lax.axis_index("dp")
    c = lax.axis_index("cp")
    x, y, q = c // 4, (c // 2) % 2, c % 2
    head = 8 * y + 2 * x + q
    mate = x * 4 + y * 2 + (1 - q)

    barrier = pltpu.get_barrier_semaphore()
    z, low_y = r // 2, r % 2
    beside = z * 2 + 1 - low_y
    y_mate = x * 4 + (1 - y) * 2 + q

    def greet(rd, cd):
        pl.semaphore_signal(barrier, inc=1, device_id=(rd, cd), device_id_type=MESH)

    for dz in FAR:
        greet(((z + dz) % 8) * 2 + low_y, c)
    greet(beside, c)
    greet(beside, y_mate)
    for d in range(1, N_CP):
        greet(r, (c + d) % N_CP)

    own = pl.ds(head * DH, DH)
    own_kv = pl.ds((head // 4) * DH, DH)
    kv_hbm = (k_hbm, v_hbm)
    loads = [
        pltpu.make_async_copy(o_hbm, o_v, lsem.at[0]),
        pltpu.make_async_copy(g_hbm, g_v, lsem.at[1]),
        pltpu.make_async_copy(lse_hbm, lse_v, lsem.at[11]),
        pltpu.make_async_copy(x_hbm, x_v, lsem.at[2]),
        pltpu.make_async_copy(cos_hbm, cos_v, lsem.at[3]),
        pltpu.make_async_copy(sin_hbm, sin_v, lsem.at[4]),
        pltpu.make_async_copy(q_hbm.at[:, own], qbuf.at[c], lsem.at[5]),
        pltpu.make_async_copy(g_hbm.at[:, own], gbuf.at[c], lsem.at[6]),
    ]
    for load in loads:
        load.start()
    for core in range(2):

        @pl.when(q == core)
        def _():
            pltpu.make_async_copy(kv_hbm[core].at[:, own_kv], kvbuf_in.at[c], lsem.at[7]).start()

    pl.semaphore_wait(barrier, (N_CP - 1) + len(FAR) + 2)

    def row_peer(d):
        xd, yd, qd = (x + d // 4) % 4, (y + (d // 2) % 2) % 2, (q + d % 2) % 2
        return xd, yd, qd, xd * 4 + yd * 2 + qd

    def remote(src, dst, send, recv, rd, cd):
        return pltpu.make_async_remote_copy(
            src_ref=src, dst_ref=dst, send_sem=send, recv_sem=recv, device_id=(rd, cd), device_id_type=MESH
        )

    def take(ref, sem):
        pltpu.make_async_copy(ref, ref, sem).wait()

    first = first_ref[0, 0]
    span = span_ref[0, 0]
    length = length_ref[0, 0]
    row_id = lax.broadcasted_iota(jnp.int32, (8, T), 0)
    tag_src[...] = jnp.where(row_id == 0, first + span, jnp.where(row_id == 1, first, 0))
    for d in ORDER:
        xd, yd, qd, cd = row_peer(d)
        kv_cols = pl.ds((2 * yd + xd // 2) * DH, DH)
        for core in range(2):

            @pl.when(qd == core)
            def _():
                remote(kv_hbm[core].at[:, kv_cols], kvbuf_in.at[c], asem_s.at[1], asem_r.at[1], r, cd).start()

        remote(tag_src, tagbuf.at[c], asem_s.at[4], asem_r.at[4], r, cd).start()

    def send_heads(ref, buf, i):
        for d in ORDER:
            xd, yd, qd, cd = row_peer(d)
            cols = pl.ds((8 * yd + 2 * xd + qd) * DH, DH)
            remote(ref.at[:, cols], buf.at[c], asem_s.at[i], asem_r.at[i], r, cd).start()

    send_heads(q_hbm, qbuf, 0)

    pos = span * T + lax.broadcasted_iota(jnp.int32, (1, T), 1)
    low = jnp.where(pos < length, first * T, 2 * N_CP * T).astype(F32)
    for load in loads[:3]:
        load.wait()
    lse_t = jnp.concatenate([lse_v[...] * LOG2E, jnp.zeros((T, T - 16), F32)], axis=1).T
    lane = lax.broadcasted_iota(jnp.int32, (T, T), 1)
    delta = jnp.zeros((T, T), F32)
    for h in range(16):
        cols = slice(h * DH, (h + 1) * DH)
        part = jnp.sum(o_v[:, cols].astype(F32) * g_v[:, cols].astype(F32), axis=1, keepdims=True)
        delta = jnp.where(lane == h, part, delta)
    delta_t = delta.T
    for h in range(16):
        rows = jnp.concatenate([lse_t[h : h + 1], delta_t[h : h + 1], low, jnp.zeros((5, T), F32)], axis=0)
        st_src[h] = rows

    def send_stats(d, _):
        xd, yd, qd, cd = row_peer(d)
        hd = 8 * yd + 2 * xd + qd
        remote(st_src.at[hd], stbuf.at[c], asem_s.at[3], asem_r.at[3], r, cd).start()
        return 0

    lax.fori_loop(1, N_CP, send_stats, 0)
    send_heads(g_hbm, gbuf, 2)
    stbuf[c] = st_src[head]
    tagbuf[c] = tag_src[...]

    loads[3].wait()

    def turn_x(b, _):
        for part in range(2):
            block = x_v[:, pl.ds(pl.multiple_of(b * 256 + part * 128, 128), 128)].T
            for k in range(8):
                owner = part * 8 + k
                start = (owner % 2) * 512 + (b % 2) * 256 + ((owner // 2) % 2) * 128 + (b // 2) * 16
                xts[owner // 4, pl.ds(pl.multiple_of(start, 16), 16), :] = block[k * 16 : (k + 1) * 16]
        return 0

    lax.fori_loop(0, N_DP, turn_x, 0)

    take(tagbuf.at[pl.ds(0, N_CP - 1)], asem_r.at[4])
    tag_load = pltpu.make_async_copy(tagbuf, tags_s, lsem.at[8])
    tag_load.start()
    tag_load.wait()
    place = [tags_s[m, 0, 0] for m in range(N_CP)]
    member = []
    for p in range(N_CP):
        m = jnp.int32(0)
        for i in range(1, N_CP):
            m = jnp.where(place[i] == p, i, m)
        member.append(m)
        sig_s[p] = p - tags_s[m, 1, 0]

    pltpu.make_async_copy(kvbuf_in.at[c], kvbuf_in.at[c], lsem.at[7]).wait()
    take(kvbuf_in.at[pl.ds(0, N_CP - 1)], asem_r.at[1])
    for p in range(N_CP):
        kvs[q, p] = kvbuf_in[member[p]]
    forward = remote(kvs.at[q], kvs.at[q], lsem.at[9], lsem.at[10], r, mate)
    forward.start()

    for load in loads[4:7]:
        load.wait()
    take(qbuf.at[pl.ds(0, N_CP - 1)], asem_r.at[0])
    take(stbuf.at[pl.ds(0, N_CP - 1)], asem_r.at[3])
    for p in range(N_CP):
        qs[p] = qbuf[member[p]]
        st_s[p // NT, :, (p % NT) * T : (p % NT + 1) * T] = stbuf[member[p]]
    forward.wait()
    for p in range(N_CP):
        kts[p // NT, :, (p % NT) * T : (p % NT + 1) * T] = kvs[0, p].T
    dqt[...] = jnp.zeros_like(dqt)

    def prob_block(kb, _):
        key = kvs[0, pl.ds(NT * kb, NT)].reshape(BL, DH)

        def unit(qb, diagonal):
            query = qs[pl.ds(NT * qb, NT)].reshape(BL, DH)
            stats = st_s[qb]
            scores = dot(key, query, 1, 1)
            s_at = lax.broadcasted_iota(jnp.int32, (BL, BL), 0)
            allowed = s_at >= stats[2:3].astype(jnp.int32) - kb * BL
            if diagonal:
                allowed = allowed & (s_at <= lax.broadcasted_iota(jnp.int32, (BL, BL), 1))
            pbuf[kb * NB + qb] = jnp.where(allowed, jnp.exp2(scores * (SCALE * LOG2E) - stats[0:1]), 0.0)
            return 0

        unit(kb, True)
        return lax.fori_loop(kb + 1, NB, lambda qb, t: unit(qb, False), 0)

    lax.fori_loop(0, NB, prob_block, 0)
    loads[7].wait()
    take(gbuf.at[pl.ds(0, N_CP - 1)], asem_r.at[2])

    def x_slot(xs, ys):
        return xbuf.at[:, pl.ds(pl.multiple_of((xs * 2 + ys) * T, T), T)]

    x_sends = [
        remote(xts.at[(x + d) % 4], x_slot(x, y), xsem_s.at[i], xsem_r.at[i], r, ((x + d) % 4) * 4 + y * 2 + q)
        for i, d in enumerate((1, 3, 2))
    ]
    for send in x_sends:
        send.start()
    keep = pltpu.make_async_copy(xts.at[x], x_slot(x, y), lsem.at[0])
    keep.start()
    across = [remote(xts.at[x], x_slot(x, y), xsem_s.at[3], xsem_r.at[3], r, y_mate)]
    across[0].start()

    def hand_on(i):
        slot = x_slot((x - (1, 3, 2)[i]) % 4, y)
        x_sends[i].wait_recv()
        across.append(remote(slot, slot, xsem_s.at[4 + i], xsem_r.at[4 + i], r, y_mate))
        across[-1].start()

    for p in range(N_CP):
        gs[p] = gbuf[member[p]]

    g, u = x // 2, x % 2
    pair_dev, other_dev = (x + 1 - 2 * u) * 4 + y * 2 + q, (3 - x) * 4 + y * 2 + q
    chunks = [pl.ds(k * 2 * T, 2 * T) for k in range(4)]
    to_mate, to_pair, to_other = {}, {}, {}

    def sum_mate(part):
        for k in range(4):
            for i in range(2):
                e = 2 * k + i
                core_src[part, pl.ds(e * T, T), :] = dkv_s[part, tags_s[2 * e + (1 - q), 0, 0]]
            to_mate[part, k] = remote(
                core_src.at[part, chunks[k]], core_buf.at[part, chunks[k]],
                ksem_s.at[0, part, k], ksem_r.at[0, part, k], r, mate,
            )
            to_mate[part, k].start()

    def chip_sum(part, k):
        own_part = [dkv_s[part, tags_s[2 * (2 * k + i) + q, 0, 0]].astype(F32) for i in range(2)]
        return jnp.concatenate(own_part, axis=0) + core_buf[part, chunks[k], :].astype(F32)

    def sum_pair(part):
        for k in range(4):
            to_mate[part, k].wait_recv()
            pair_src[part, chunks[k], :] = chip_sum(part, k).astype(BF16)
            to_pair[part, k] = remote(
                pair_src.at[part, chunks[k]], pair_buf.at[part, chunks[k]],
                ksem_s.at[1, part, k], ksem_r.at[1, part, k], r, pair_dev,
            )
            to_pair[part, k].start()

    def share(part):
        for k in range(4):
            to_pair[part, k].wait_recv()
            lanes = pl.ds(pl.multiple_of(g * DH, DH), DH)
            total = chip_sum(part, k) + pair_buf[part, chunks[k], :].astype(F32)
            kvbuf[part, chunks[k], lanes] = total.astype(BF16)
            done = kvbuf.at[part, chunks[k], lanes]
            to_other[part, k] = remote(
                done, done, ksem_s.at[2, part, k], ksem_r.at[2, part, k], r, other_dev
            )
            to_other[part, k].start()

    def value_block(kb, _):
        def unit(qb, dv):
            grad = gs[pl.ds(NT * qb, NT)].reshape(BL, DH)
            return dv + dot(pbuf[kb * NB + qb].astype(BF16), grad, 1, 0)

        dv = lax.fori_loop(kb, NB, unit, jnp.zeros((BL, DH), F32))
        for i in range(NT):
            dkv_s[0, NT * kb + i] = dv[i * T : (i + 1) * T].astype(BF16)
        return 0

    def key_block(step, _):
        kb = NB - 1 - step
        value = kvs[1, pl.ds(NT * kb, NT)].reshape(BL, DH)
        key_t = kts[kb]

        def unit(qb, dk):
            query = qs[pl.ds(NT * qb, NT)].reshape(BL, DH)
            grad = gs[pl.ds(NT * qb, NT)].reshape(BL, DH)
            dp = dot(value, grad, 1, 1)
            ds = (pbuf[kb * NB + qb] * (dp - st_s[qb][1:2])).astype(BF16)
            dqt[qb] += dot(key_t, ds, 1, 0)
            return dk + dot(ds, query, 1, 0)

        dk = lax.fori_loop(kb, NB, unit, jnp.zeros((BL, DH), F32))
        for i in range(NT):
            p = NT * kb + i
            turned = dk[i * T : (i + 1) * T] * SCALE
            sig = sig_s[p]
            plain = turned * cos_v[sig] + pltpu.roll(turned, DH // 2, 1) * sin_v[sig]
            dkv_s[1, p] = plain.astype(BF16)
        return 0

    lax.fori_loop(0, NB, value_block, 0)
    sum_mate(0)
    lax.fori_loop(0, 2, key_block, 0)
    sum_pair(0)
    lax.fori_loop(2, 3, key_block, 0)
    hand_on(0)
    hand_on(1)
    lax.fori_loop(3, NB, key_block, 0)
    sum_mate(1)
    share(0)
    sum_pair(1)
    hand_on(2)

    for p in range(N_CP):
        dq_s[p] = (dqt[p // NT, :, (p % NT) * T : (p % NT + 1) * T] * SCALE).T.astype(BF16)
    for m in range(N_CP):
        dq_src[m] = dq_s[place[m]]

    share(1)


    def send_dq(d, _):
        xd, yd, qd, cd = row_peer(d)
        remote(dq_src.at[cd], dq_out.at[:, own], dsem_s, dsem_r, r, cd).start()
        return 0

    keep.wait()
    for send in across:
        send.wait_recv()

    def tile(start, part):
        return dot(xbuf[pl.ds(pl.multiple_of(start, 512), 512), :], kvbuf[part], 1, 0).reshape(4, 128, 256)

    def tile_mate(part):
        for k in range(4):
            to_other[part, k].wait_recv()
        w_src[part] = tile((1 - q) * 512, part).astype(BF16)
        w_mates[part] = remote(w_src.at[part], w_core.at[part], wsem_s.at[part], wsem_r.at[part], r, mate)
        w_mates[part].start()

    def tile_own(part):
        w_own[part] = tile(q * 512, part)

    def send_y(part, half):
        cols = slice(half * DH, (half + 1) * DH)
        if half == 0:
            w_mates[part].wait_recv()
        total = w_own[part, :, :, cols] + w_core[part, :, :, cols].astype(F32)
        j = 2 * part + half
        w_sum[j] = total
        ysend[j] = total.astype(BF16)
        for dl, dy in ((0, 1), (1, 1), (1, 0)):
            yl, yo = (low_y + dl) % 2, (y + dy) % 2
            remote(
                ysend.at[j, 2 * yl + yo], ybuf.at[j, 2 * low_y + y],
                ysem_s.at[j], ysem_r.at[j], z * 2 + yl, x * 4 + yo * 2 + q,
            ).start()

    def send_z(j):
        take(ybuf.at[j, pl.ds(0, 3)], ysem_r.at[j])
        near = w_sum[j, 2 * low_y + y] + ybuf[j, 2 * (1 - low_y) + y].astype(F32)
        far = ybuf[j, 1 - y].astype(F32) + ybuf[j, 3 - y].astype(F32)
        zsend[j, :, y] = near.astype(BF16).reshape(8, 16, DH)
        zsend[j, :, 1 - y] = far.astype(BF16).reshape(8, 16, DH)
        for dz in FAR:
            zd = (z + dz) % 8
            remote(zsend.at[j, zd], zbuf.at[j, z], zsem_s.at[j], zsem_r.at[j], zd * 2 + low_y, c).start()
        zbuf[j, z] = zsend[j, z]

    def finish(j):
        take(zbuf.at[j, pl.ds(0, 7)], zsem_r.at[j])
        total = zbuf[j, 0].astype(F32)
        for i in range(1, 8):
            total = total + zbuf[j, i].astype(F32)
        for yy in range(2):
            start = 512 * (1 - j // 2) + 256 * yy + DH * (j % 2)
            w_out[:, start : start + DH] = total[yy].astype(BF16)

    w_mates = {}
    for d in HOME[0]:
        send_dq(d, 0)
    tile_mate(0)
    tile_own(0)
    tile_mate(1)
    send_y(0, 0)
    send_y(0, 1)
    tile_own(1)
    send_y(1, 0)
    send_y(1, 1)
    send_z(0)
    for d in HOME[1]:
        send_dq(d, 0)
    dq_keep = pltpu.make_async_copy(dq_src.at[c], dq_out.at[:, own], lsem.at[2])
    dq_keep.start()
    send_z(1)
    send_z(2)
    send_z(3)
    for j in range(4):
        finish(j)

    for sends in (to_mate, to_pair, to_other):
        for send in sends.values():
            send.wait_send()
    take(dq_src.at[pl.ds(0, N_CP - 1)], dsem_r)
    take(dq_src.at[pl.ds(0, N_CP - 1)], dsem_s)
    dq_keep.wait()
    for i, buf in enumerate((qbuf, kvbuf_in, gbuf, stbuf, tagbuf)):
        take(buf.at[pl.ds(0, N_CP - 1)], asem_s.at[i])
    for send in x_sends + across:
        send.wait_send()
    for part in range(2):
        w_mates[part].wait_send()
    for j in range(4):
        take(ybuf.at[j, pl.ds(0, 3)], ysem_s.at[j])
        take(zbuf.at[j, pl.ds(0, 7)], zsem_s.at[j])


def shards(layer_input, queries, keys, values, outputs, out_grad, log_sum_exp, group_first, span_index, seq_length):
    cos_table, sin_table = rope_tables()
    anywhere = pl.BlockSpec(memory_space=pl.ANY)
    vmem = pl.BlockSpec(memory_space=pltpu.VMEM)
    smem = pl.BlockSpec(memory_space=pltpu.SMEM)
    dma = pltpu.SemaphoreType.DMA
    V = pltpu.VMEM
    scratch = [
        V((T, 4096), BF16), V((T, 2048), BF16), V((T, 2048), BF16), V((T, 16), F32), V((16, T, DH), F32), V((16, T, DH), F32),
        V((16, T, DH), BF16), V((16, T, DH), BF16), V((16, T, DH), BF16),
        V((16, 8, T), F32), V((16, 8, T), jnp.int32), V((16, 8, T), F32), V((8, T), jnp.int32),
        pltpu.SMEM((16, 8, T), jnp.int32), pltpu.SMEM((16,), jnp.int32),
        V((16, T, DH), BF16), V((16, T, DH), BF16), V((2, 16, T, DH), BF16),
        V((NB, DH, BL), BF16), V((NB, 8, BL), F32), V((NB, DH, BL), F32), V((2, 16, T, DH), BF16),
        V((NB * NB, BL, BL), F32), V((4, 1024, T), BF16), V((1024, 1024), BF16), V((2, 1024, DH), BF16),
        V((2, 1024, DH), BF16), V((2, 1024, DH), BF16), V((2, 1024, DH), BF16), V((2, 1024, 256), BF16),
        V((16, T, DH), BF16), V((16, T, DH), BF16), V((2, 4, T, 256), BF16), V((2, 4, T, 256), BF16),
        V((2, 4, T, 256), F32), V((4, 4, T, DH), F32), V((4, 4, T, DH), BF16), V((4, 4, T, DH), BF16),
        V((4, 8, 2, 16, DH), BF16), V((4, 8, 2, 16, DH), BF16),
        dma((12,)), dma((5,)), dma((5,)), dma((7,)), dma((7,)), dma((3, 2, 4)), dma((3, 2, 4)), dma((2,)), dma((2,)), dma, dma,
        dma((4,)), dma((4,)), dma((4,)), dma((4,)),
    ]
    return pl.pallas_call(
        kernel,
        out_shape=(
            jax.ShapeDtypeStruct((T, 2048), BF16),
            jax.ShapeDtypeStruct((16, 1024), BF16),
        ),
        in_specs=[anywhere] * 7 + [smem, smem, smem, anywhere, anywhere],
        out_specs=(anywhere, vmem),
        scratch_shapes=scratch,
        compiler_params=pltpu.CompilerParams(
            collective_id=0, has_side_effects=True, vmem_limit_bytes=62 * 1024 * 1024
        ),
        name="attention_backward",
    )(
        layer_input, queries, keys, values, outputs, out_grad, log_sum_exp,
        group_first, span_index, seq_length, jnp.asarray(cos_table), jnp.asarray(sin_table),
    )


def solution(mesh):
    both = P(("dp", "cp"), None)
    placed = (both,) * 7 + (P("dp", "cp"),) * 3
    return jax.shard_map(shards, mesh=mesh, in_specs=placed, out_specs=(both, both), check_vma=False)
```
